32 devices in a mesh: gx: 8 (over z, y), gy: 4 (over x, core).
Axes of the slice: x: 2, y: 2, z: 4, core: 2. Of those that a mesh axis runs over, the one named last changes fastest.
Arguments:
- cot_u: float32 [30, 1024, 1024], P(None, 'gy', 'gx'), may hold values from -6 to 6
- cot_v: float32 [30, 1024, 1024], P(None, 'gy', 'gx'), may hold values from -6 to 6
- cot_t: float32 [30, 1024, 1024], P(None, 'gy', 'gx'), may hold values from -6 to 6
- levels: int32 [1024, 1024], P('gy', 'gx'), may hold values from 0 to 30
- mixing: float32 [1024, 1024], P('gy', 'gx'), may hold values from 0.02 to 0.12
- pattern_x: int32 [8, 3], replicated, may hold values from 0 to 7, all different within a row
- blocks_x: float32 [8, 3, 128, 128], replicated, may hold values from -0.3125 to 0.3125
- pattern_y: int32 [8, 3], replicated, may hold values from 0 to 7, all different within a row
- blocks_y: float32 [8, 3, 128, 128], replicated, may hold values from -0.3125 to 0.3125
Outputs:
- grad_u: float32 [30, 1024, 1024], P(None, 'gy', 'gx')
- grad_v: float32 [30, 1024, 1024], P(None, 'gy', 'gx')
- grad_t: float32 [30, 1024, 1024], P(None, 'gy', 'gx')
- forcing_update: float32 [3, 1024, 1024], P(None, 'gy', 'gx')
The draws below stay inside these ranges and needn't reach their ends.
Inputs may be any that keep to these rules, and one draw needn't show every extreme that they name: `pattern_x`: each block row names 3 different block columns, and every block column is named by some row. `pattern_y`: each block row names 3 different block columns, and every block column is named by some row.
All inputs are finite; a program needn't handle non-finite values.
Results may differ from the reference program's by a relative error of at most 0.00007.
Values sent between devices are 32-bit elements; how exact they have to be, the bound alone decides.
No kernel may reach another device: no remote copies, remote signals or barrier semaphores. Data moves between devices by JAX's collectives and lax.ppermute only.
A program may use at most 384 MiB of HBM per device.

```python
import math
import jax
import jax.numpy as jnp
from jax import lax

K = 30
BLOCK = 128
NNZ = 3
NX = 1024
NY = 1024
NBX = 8
NBY = 8


def place_ends(values, own_key, least, high):
    index_at = [jax.random.randint(jax.random.fold_in(own_key, axis), (), 0, length) for axis, length in enumerate(values.shape)]
    longest = values.shape.index(max(values.shape))
    next_to = index_at[:longest] + [(index_at[longest] + 1) % values.shape[longest]] + index_at[longest + 1:]
    return values.at[tuple(index_at)].set(least).at[tuple(next_to)].set(high)


def block_levels(own_key, extent, pieces, least, high):
    level, own = 1.0, jax.random.fold_in(own_key, 6)
    for dim, shards_of in pieces:
        heights = jnp.exp(jax.random.uniform(jax.random.fold_in(own, dim), (shards_of,), jnp.float32, least / len(pieces), high / len(pieces)))
        level = level * jnp.repeat(heights, extent[dim] // shards_of).reshape([-1 if axis == dim else 1 for axis in range(len(extent))])
    return level


def choose_distinct(own_key, rows, number_of, top, lift):
    sequence = jax.random.permutation(jax.random.fold_in(own_key, 1), number_of)
    boost = sequence
    for power in range(3):
        boost = boost * boost // number_of
    boost = boost * lift // number_of
    tickets = jax.random.randint(jax.random.fold_in(own_key, 2), (rows, number_of), 0, 4096) + boost
    fixed_rows = jax.random.permutation(jax.random.fold_in(own_key, 3), rows)[jnp.arange(number_of) % rows]
    tickets = jnp.where(jnp.arange(rows)[:, None] == fixed_rows[None, :], 1 << 14, tickets)
    score = tickets * number_of + jnp.arange(number_of)
    return lax.top_k(score.astype(jnp.int32), top)[1].astype(jnp.int32)


def gaussian(rng, shape, spread, most, shards=(), kind=jnp.bfloat16):
    gain = block_levels(rng, shape, shards, -0.22, 0.18) if shards else 1.0
    array = jax.random.normal(rng, shape, jnp.float32) * spread * gain
    return jnp.minimum(jnp.maximum(array, -most), most).astype(kind)


def setup_inputs(seed: int = 0) -> dict:
    key_list = jax.random.split(jax.random.key(seed), 10)
    return {
        "cot_u": gaussian(key_list[0], (K, NY, NX), 1.0, 6.0, ((1, 4), (2, 8)), jnp.float32),
        "cot_v": gaussian(key_list[1], (K, NY, NX), 1.0, 6.0, ((1, 4), (2, 8)), jnp.float32),
        "cot_t": gaussian(key_list[2], (K, NY, NX), 1.0, 6.0, ((1, 4), (2, 8)), jnp.float32),
        "levels": place_ends(jax.random.randint(key_list[3], (NY, NX), 0, K + 1), jax.random.fold_in(key_list[3], 1), 0, K).astype(jnp.int32),
        "mixing": jnp.clip(jnp.exp(math.log(0.12) - 1.7917595 * jax.random.uniform(key_list[4], (NY, NX), jnp.float32) ** block_levels(key_list[4], (NY, NX), ((0, 4), (1, 8)), -0.2, 0.2)), 0.02, 0.12),
        "pattern_x": choose_distinct(key_list[5], NBX, NBX, NNZ, 0),
        "blocks_x": gaussian(key_list[6], (NBX, NNZ, BLOCK, BLOCK), (BLOCK * NNZ) ** -0.5, 0.3125, (), jnp.float32),
        "pattern_y": choose_distinct(key_list[7], NBY, NBY, NNZ, 0),
        "blocks_y": gaussian(key_list[8], (NBY, NNZ, BLOCK, BLOCK), (BLOCK * NNZ) ** -0.5, 0.3125, (), jnp.float32),
    }


time_step = 0.5
gravity_scale = 0.05
coriolis_base = 0.4
zonal_slope = 0.3
north_slope = 0.2

def shifted(field, step_y, step_x):
    height = field.shape[-2] - 2
    width = field.shape[-1] - 2
    return field[..., 1 + step_y:1 + step_y + height, 1 + step_x:1 + step_x + width]

def laplace(field):
    return shifted(field, 0, 1) + shifted(field, 0, -1) + shifted(field, 1, 0) + shifted(field, -1, 0) - 4.0 * shifted(field, 0, 0)

def advance(vel_u, vel_v, tracer, stress_x, stress_y, heat_flux, depth_wet, mixing, coriolis):
    depth = vel_u.shape[0]
    layer = lax.broadcasted_iota(jnp.int32, (depth, 1, 1), 0).astype(jnp.float32)
    wet = jnp.where(layer < depth_wet[None], 1.0, 0.0).astype(vel_u.dtype)
    surface = jnp.where(layer < 0.5, 1.0, 0.0).astype(vel_u.dtype)
    wet_c = shifted(wet, 0, 0)
    wet_u = wet_c * shifted(wet, 0, -1)
    wet_v = wet_c * shifted(wet, -1, 0)
    press = gravity_scale * jnp.cumsum(tracer, axis=0)
    diffuse = shifted(mixing, 0, 0)
    v_mean = 0.25 * (shifted(vel_v, 0, 0) + shifted(vel_v, 1, 0) + shifted(vel_v, 0, -1) + shifted(vel_v, 1, -1))
    u_mean = 0.25 * (shifted(vel_u, 0, 0) + shifted(vel_u, 0, 1) + shifted(vel_u, -1, 0) + shifted(vel_u, -1, 1))
    new_u = wet_u * (shifted(vel_u, 0, 0) + time_step * (coriolis * v_mean - (shifted(press, 0, 0) - shifted(press, 0, -1))) + diffuse * laplace(vel_u))
    new_v = wet_v * (shifted(vel_v, 0, 0) + time_step * (-coriolis * u_mean - (shifted(press, 0, 0) - shifted(press, -1, 0))) + diffuse * laplace(vel_v))
    u_cell = 0.5 * (shifted(vel_u, 0, 0) + shifted(vel_u, 0, 1))
    v_cell = 0.5 * (shifted(vel_v, 0, 0) + shifted(vel_v, 1, 0))
    new_t = wet_c * (shifted(tracer, 0, 0) - time_step * (zonal_slope * u_cell + north_slope * v_cell) + diffuse * laplace(tracer))
    new_u = new_u + surface * wet_u * time_step * stress_x
    new_v = new_v + surface * wet_v * time_step * stress_y
    new_t = new_t + surface * wet_c * time_step * heat_flux
    return (new_u, new_v, new_t)

def along_last(field, pattern, blocks):
    lead = field.shape[:-1]
    block = blocks.shape[-1]
    grouped = field.reshape(lead + (field.shape[-1] // block, block))
    picked = jnp.take(grouped, pattern, axis=-2)
    result = jnp.einsum('crnjb,njab->crna', picked, blocks, precision=lax.Precision.HIGHEST)
    return result.reshape(lead + (pattern.shape[0] * block,))

def along_rows(field, pattern, blocks):
    comps, total, width = field.shape
    block = blocks.shape[-1]
    grouped = field.reshape(comps, total // block, block, width)
    picked = jnp.take(grouped, pattern, axis=1)
    result = jnp.einsum('cnjbw,njab->cnaw', picked, blocks, precision=lax.Precision.HIGHEST)
    return result.reshape(comps, pattern.shape[0] * block, width)

def reference(cot_u, cot_v, cot_t, levels, mixing, pattern_x, blocks_x, pattern_y, blocks_y):
    depth, rows, cols = cot_u.shape
    depth_wet = jnp.pad(levels.astype(jnp.float32), 1)
    diffusion = jnp.pad(mixing, 1)
    lines = jnp.arange(rows, dtype=jnp.int32).astype(jnp.float32)
    coriolis = (coriolis_base * (0.5 + (lines + 0.5) / rows))[:, None]
    zero_field = jnp.zeros((depth, rows + 2, cols + 2), jnp.float32)
    zero_plane = jnp.zeros((rows, cols), jnp.float32)

    def forward(vel_u, vel_v, tracer, stress_x, stress_y, heat_flux):
        return advance(vel_u, vel_v, tracer, stress_x, stress_y, heat_flux, depth_wet, diffusion, coriolis)
    _, pullback = jax.vjp(forward, zero_field, zero_field, zero_field, zero_plane, zero_plane, zero_plane)
    grad_u, grad_v, grad_t, grad_sx, grad_sy, grad_q = pullback((cot_u, cot_v, cot_t))
    surface = jnp.stack([grad_sx, grad_sy, grad_q])
    mixed = along_last(surface, pattern_x, blocks_x)
    mixed = along_rows(mixed, pattern_y, blocks_y)
    return (grad_u[:, 1:-1, 1:-1], grad_v[:, 1:-1, 1:-1], grad_t[:, 1:-1, 1:-1], mixed)
```

```python
import functools

import jax
import jax.numpy as jnp
from jax import lax
from jax.experimental import pallas as pl
from jax.experimental.pallas import tpu as pltpu
from jax.sharding import PartitionSpec as P

time_step = 0.5
gravity_scale = 0.05
coriolis_base = 0.4
zonal_slope = 0.3
north_slope = 0.2

LANES = 128
GROUP = 8
F32 = jnp.float32
BF16 = jnp.bfloat16
VMEM_LIMIT = 48 * 1024 * 1024


def whole():
    return pl.BlockSpec(memory_space=pltpu.VMEM)


def anywhere():
    return pl.BlockSpec(memory_space=pl.ANY)


def smem():
    return pl.BlockSpec(memory_space=pltpu.SMEM)


def struct(*shape):
    return jax.ShapeDtypeStruct(shape, F32)


def params(**kwargs):
    return pltpu.CompilerParams(vmem_limit_bytes=VMEM_LIMIT, **kwargs)


def cost(microseconds):
    return pl.CostEstimate(
        flops=int(microseconds * 1e6), bytes_accessed=int(microseconds * 3.0e6), transcendentals=0
    )


def lane_ids(shape):
    return lax.broadcasted_iota(jnp.int32, shape, 1)


def row_ids(shape):
    return lax.broadcasted_iota(jnp.int32, shape, 0)


def edge_kernel(levels_ref, col_ref, row_ref):
    rows, cols = levels_ref.shape
    field = levels_ref[...].astype(F32)
    col_ref[...] = jnp.transpose(field)[cols - GROUP :]
    row_ref[...] = field[rows - GROUP :]


def edges(levels):
    rows, cols = levels.shape
    return pl.pallas_call(
        edge_kernel,
        out_shape=(struct(GROUP, rows), struct(GROUP, cols)),
        in_specs=[whole()],
        out_specs=(whole(), whole()),
        compiler_params=params(),
        cost_estimate=cost(1.0),
        name="edges",
    )(levels)


def surface_kernel(
    levels_ref, col_ref, row_ref, u_ref, v_ref, t_ref, out_ref, wet_c_ref, wet_u_ref, wet_v_ref
):
    rows, cols = levels_ref.shape
    field = levels_ref[...].astype(F32)
    lane = lane_ids(field.shape)
    row = row_ids(field.shape)
    col = jnp.broadcast_to(jnp.transpose(col_ref[...])[:, GROUP - 1 :], field.shape)
    west = jnp.where(lane == 0, col, pltpu.roll(field, 1, 1))
    line = jnp.broadcast_to(row_ref[GROUP - 1 :, :], field.shape)
    south = jnp.where(row == 0, line, pltpu.roll(field, 1, 0))
    wet_u = jnp.minimum(field, west)
    wet_v = jnp.minimum(field, south)
    wet_c_ref[...] = field
    wet_u_ref[...] = wet_u
    wet_v_ref[...] = wet_v
    parts, chunk = (out_ref.shape[0], out_ref.shape[1] // 3)
    for comp, (ref, wet) in enumerate(((u_ref, wet_u), (v_ref, wet_v), (t_ref, field))):
        grad = jnp.where(wet > 0.0, time_step * ref[0], 0.0)
        for part in range(parts):
            out_ref[part, comp * chunk : (comp + 1) * chunk, :] = grad[
                part * chunk : (part + 1) * chunk
            ]


def surface(levels, col, row, cot_u, cot_v, cot_t, parts):
    rows, cols = levels.shape
    top = pl.BlockSpec((1, rows, cols), lambda i: (0, 0, 0))

    def full(*shape):
        return pl.BlockSpec(shape, lambda i: (0,) * len(shape))

    out = (parts, 3 * rows // parts, cols)
    return pl.pallas_call(
        surface_kernel,
        grid=(1,),
        out_shape=(struct(*out),) + (struct(rows, cols),) * 3,
        in_specs=[full(rows, cols), full(GROUP, rows), full(GROUP, cols), top, top, top],
        out_specs=(full(*out),) + (full(rows, cols),) * 3,
        compiler_params=params(),
        cost_estimate=cost(1.5),
        name="surface",
    )(levels, col, row, cot_u, cot_v, cot_t)


def rim_kernel(
    step,
    wet_c_ref,
    wet_u_ref,
    wet_v_ref,
    mix_ref,
    u_ref,
    v_ref,
    t_ref,
    east_ref,
    west_ref,
    north_ref,
    south_ref,
    corner_e_ref,
    corner_w_ref,
):
    at = pl.program_id(0)
    depth = pl.num_programs(0) * step
    rows, cols = mix_ref.shape
    slots = 3 * depth
    first = at * step
    chunk = 2 * GROUP
    lane = lane_ids((chunk, cols))

    @pl.when(at == 0)
    def _():
        mix = mix_ref[...]
        rolled = pltpu.roll(mix, slots + 1, 1)
        ids = lane_ids(mix.shape)
        east_ref[...] = jnp.where(ids == slots, rolled, 0.0)
        west_ref[...] = jnp.where(ids == slots + 1, rolled, 0.0)
        north_ref[slots:, :] = jnp.broadcast_to(
            mix[rows - 1 :], (north_ref.shape[0] - slots, cols)
        )
        south_ref[slots:, :] = jnp.broadcast_to(mix[:1], (south_ref.shape[0] - slots, cols))

    fields = ((u_ref, wet_u_ref), (v_ref, wet_v_ref), (t_ref, wet_c_ref))

    def body(i, carry):
        base = pl.multiple_of(i * chunk, chunk)
        here = pl.ds(base, chunk)
        east = east_ref[here, :]
        west = west_ref[here, :]
        wets = [wet[here, :] for _, wet in fields]
        for k in range(step):
            level = (first + k).astype(F32)
            for f, (ref, _) in enumerate(fields):
                slot = 3 * (first + k) + f
                value = jnp.where(level < wets[f], ref[k, here, :], 0.0)
                rolled = pltpu.roll(value, slot + 1, 1)
                east = jnp.where(lane == slot, rolled, east)
                west = jnp.where(lane == slot + 1, rolled, west)
        east_ref[here, :] = east
        west_ref[here, :] = west
        return carry

    lax.fori_loop(0, rows // chunk, body, 0)
    for k in range(step):
        level = (first + k).astype(F32)
        for f, (ref, wet) in enumerate(fields):
            slot = 3 * (first + k) + f
            for line, out in ((rows - 1, north_ref), (0, south_ref)):
                value = jnp.where(
                    level < wet[line : line + 1, :], ref[k, line : line + 1, :], 0.0
                )
                out[pl.ds(slot, 1), :] = value

    @pl.when(at == pl.num_programs(0) - 1)
    def _():
        corner_e_ref[...] = east_ref[:GROUP, :]
        corner_w_ref[...] = west_ref[rows - GROUP :, :]


def rims(wet_c, wet_u, wet_v, mixing, cot_u, cot_v, cot_t, after):
    depth, rows, cols = cot_u.shape
    step = 3
    lines = -(-(3 * depth + 1) // GROUP) * GROUP

    def full(*shape):
        return pl.BlockSpec(shape, lambda i: (0,) * len(shape))

    plane = full(rows, cols)
    block = pl.BlockSpec((step, rows, cols), lambda i: (i, 0, 0))

    def kernel(*refs):
        rim_kernel(step, *refs[:7], *refs[8:])

    return pl.pallas_call(
        kernel,
        grid=(depth // step,),
        out_shape=(struct(rows, cols),) * 2
        + (struct(lines, cols),) * 2
        + (struct(GROUP, cols),) * 2,
        in_specs=[plane] * 4 + [block] * 3 + [anywhere()],
        out_specs=(plane,) * 2 + (full(lines, cols),) * 2 + (full(GROUP, cols),) * 2,
        compiler_params=params(),
        cost_estimate=cost(5.0),
        name="rims",
    )(wet_c, wet_u, wet_v, mixing, cot_u, cot_v, cot_t, after)


def adjoint_kernel(
    step,
    depth,
    total_rows,
    wet_c_ref,
    wet_u_ref,
    wet_v_ref,
    mix_ref,
    hw_ref,
    he_ref,
    hn_ref,
    hs_ref,
    nw_ref,
    se_ref,
    u_ref,
    v_ref,
    t_ref,
    gu_ref,
    gv_ref,
    gt_ref,
    a_ref,
    b_ref,
    c_ref,
    mix_n_ref,
    mix_s_ref,
    keep_ref,
    cor_ref,
    pe_ref,
    pw_ref,
    sum_a_ref,
    sum_d_ref,
):
    rows, cols = mix_ref.shape
    at = pl.program_id(0)
    slots = 3 * depth
    first = depth - (at + 1) * step
    pad = GROUP
    half = 0.5 * time_step
    cor_step = coriolis_base * half * 0.5 / total_rows
    slope_u = 0.5 * time_step * zonal_slope
    slope_v = 0.5 * time_step * north_slope
    weight = time_step * gravity_scale

    @pl.when(at == 0)
    def _():
        shape = (rows, cols)
        lane = lane_ids(shape)
        row = row_ids(shape)
        start = lax.axis_index("gy") * rows
        lines = (row + start).astype(F32)
        cor = (0.25 * time_step * coriolis_base) * (0.5 + (lines + 0.5) / total_rows)
        cor_n = (0.25 * time_step * coriolis_base) * (0.5 + (lines + 1.5) / total_rows)
        cor_s = (0.25 * time_step * coriolis_base) * (0.5 + (lines - 0.5) / total_rows)
        cor_ref[...] = cor
        mix = mix_ref[...]
        keep_ref[...] = 1.0 - 4.0 * mix
        mix_n_ref[...] = jnp.where(
            row == rows - 1,
            jnp.broadcast_to(hn_ref[slots : slots + 1, :], shape),
            pltpu.roll(mix, rows - 1, 0),
        )
        mix_s_ref[...] = jnp.where(
            row == 0,
            jnp.broadcast_to(hs_ref[slots : slots + 1, :], shape),
            pltpu.roll(mix, 1, 0),
        )
        east = he_ref[...]
        kind = lax.rem(lane + 2, 3)
        mixed = east * jnp.broadcast_to(east[:, slots + 1 : slots + 2], shape)
        below = jnp.where(
            row == 0,
            jnp.broadcast_to(se_ref[GROUP - 1 :, :], shape),
            pltpu.roll(east, 1, 0),
        )
        turned = cor * east + cor_s * below
        total = jnp.where((kind == 0) & (lane <= slots), east, 0.0)
        reach = 3
        while reach < slots:
            moved = pltpu.roll(total, cols - reach, 1)
            total = total + jnp.where(lane + reach < cols, moved, 0.0)
            reach *= 2
        pe_ref[...] = (
            mixed
            + jnp.where(kind == 1, pltpu.roll(turned, 1, 1), 0.0)
            + jnp.where(kind == 2, pltpu.roll(weight * total, 2, 1), 0.0)
        )
        west = hw_ref[...]
        kind = lax.rem(lane, 3)
        mixed = west * jnp.broadcast_to(west[:, slots : slots + 1], shape)
        above = jnp.where(
            row == rows - 1,
            jnp.broadcast_to(nw_ref[:1, :], shape),
            pltpu.roll(west, rows - 1, 0),
        )
        turned = cor * west + cor_n * above
        pw_ref[...] = mixed - jnp.where(
            kind == 0,
            pltpu.roll(turned, cols - 1, 1) + pltpu.roll(slope_u * west, cols - 2, 1),
            0.0,
        )
        sum_a_ref[...] = jnp.zeros(shape, F32)
        sum_d_ref[...] = jnp.zeros(shape, F32)

    fields = (
        (u_ref, wet_u_ref, a_ref),
        (v_ref, wet_v_ref, b_ref),
        (t_ref, wet_c_ref, c_ref),
    )

    def mask(i, carry):
        base = pl.multiple_of(i * 2 * GROUP, 2 * GROUP)
        here = pl.ds(base, 2 * GROUP)
        there = pl.ds(pl.multiple_of(base + pad, GROUP), 2 * GROUP)
        wets = [wet[here, :] for _, wet, _ in fields]
        for k in range(step):
            level = (first + k).astype(F32)
            for f, (ref, _, out) in enumerate(fields):
                out[k, there, :] = jnp.where(level < wets[f], ref[k, here, :], 0.0)
        return carry

    lax.fori_loop(0, rows // (2 * GROUP), mask, 0)
    for k in range(step):
        for f, (_, _, out) in enumerate(fields):
            slot = 3 * (first + k) + f
            out[k, pad - 1 : pad, :] = hs_ref[pl.ds(slot, 1), :]
            out[k, pad + rows : pad + rows + 1, :] = hn_ref[pl.ds(slot, 1), :]

    chunk = 2 * GROUP
    lane = lane_ids((chunk, cols))
    is_east = lane == cols - 1
    is_west = lane == 0

    def body(i, carry):
        base = pl.multiple_of(i * chunk, chunk)
        here = pl.ds(base, chunk)
        center = pl.ds(base + pad, chunk)
        north = pl.ds(base + pad + 1, chunk)
        south = pl.ds(base + pad - 1, chunk)
        mix = mix_ref[here, :]
        mix_n = mix_n_ref[here, :]
        mix_s = mix_s_ref[here, :]
        keep = keep_ref[here, :]
        cor = cor_ref[here, :]
        cor_n = cor + cor_step
        cor_s = cor - cor_step
        pe = pe_ref[here, :]
        pw = pw_ref[here, :]
        sum_a = sum_a_ref[here, :]
        sum_d = sum_d_ref[here, :]
        for k in reversed(range(step)):
            slot = 3 * (first + k)

            def from_east(value, f, slot=slot):
                edge = pltpu.roll(pe, cols - 2 - (slot + f), 1)
                return jnp.where(is_east, edge, pltpu.roll(value, cols - 1, 1))

            def from_west(value, f, slot=slot):
                edge = pltpu.roll(pw, cols - (slot + f), 1)
                return jnp.where(is_west, edge, pltpu.roll(value, 1, 1))

            a = a_ref[k, center, :]
            a_n = a_ref[k, north, :]
            a_s = a_ref[k, south, :]
            b = b_ref[k, center, :]
            b_n = b_ref[k, north, :]
            b_s = b_ref[k, south, :]
            c = c_ref[k, center, :]
            c_n = c_ref[k, north, :]
            c_s = c_ref[k, south, :]
            mix_a = mix * a
            turn_b = cor * b + cor_n * b_n + slope_u * c
            gu_ref[k, here, :] = (
                keep * a
                + (mix_n * a_n + mix_s * a_s)
                - turn_b
                + (from_west(mix_a - turn_b, 0) + from_east(mix_a, 0))
            )
            mix_b = mix * b
            turn_a = cor * a + cor_s * a_s
            gv_ref[k, here, :] = (
                keep * b
                + (mix_n * b_n + mix_s * b_s)
                + (turn_a - slope_v * (c + c_s))
                + (from_west(mix_b, 1) + from_east(mix_b + turn_a, 1))
            )
            mix_c = mix * c
            sum_a = sum_a + weight * a
            sum_d = sum_d + weight * (b - b_n)
            gt_ref[k, here, :] = (
                keep * c
                + (mix_n * c_n + mix_s * c_s)
                - (sum_a + sum_d)
                + (from_west(mix_c, 2) + from_east(mix_c + sum_a, 2))
            )
        sum_a_ref[here, :] = sum_a
        sum_d_ref[here, :] = sum_d
        return carry

    lax.fori_loop(0, rows // chunk, body, 0)


def adjoint(planes, halos, cots, after, total_rows):
    depth, rows, cols = cots[0].shape
    step = 3
    steps = depth // step

    def full(*shape):
        return pl.BlockSpec(shape, lambda i: (0,) * len(shape))

    plane = full(rows, cols)
    block = pl.BlockSpec((step, rows, cols), lambda i: (steps - 1 - i, 0, 0))
    n_in = len(planes) + len(halos) + 3

    def kernel(*refs):
        adjoint_kernel(step, depth, total_rows, *refs[:n_in], *refs[n_in + 1 :])

    padded = pltpu.VMEM((step, rows + 2 * GROUP, cols), F32)
    return pl.pallas_call(
        kernel,
        grid=(steps,),
        out_shape=(struct(depth, rows, cols),) * 3,
        in_specs=[plane] * len(planes)
        + [full(*halo.shape) for halo in halos]
        + [block] * 3
        + [anywhere()],
        out_specs=(block,) * 3,
        scratch_shapes=[padded] * 3 + [pltpu.VMEM((rows, cols), F32)] * 8,
        compiler_params=params(),
        cost_estimate=cost(12.0),
        name="adjoint",
    )(*planes, *halos, *cots, after)


def halves(value):
    high = value.astype(BF16)
    return high, (value - high.astype(F32)).astype(BF16)


def zonal_kernel(
    gy_size, pattern_ref, blocks_ref, field_ref, out_ref, high_ref, low_ref
):
    tiles, height, cols = field_ref.shape
    chunk = height // 3
    width = cols // gy_size
    slots = LANES // width
    groups = chunk // GROUP
    owner = lane_ids((GROUP, cols)) // width
    for tile in range(tiles):
        high_ref[tile], low_ref[tile] = halves(field_ref[tile])
    for r in range(blocks_ref.shape[0]):
        picked = [pattern_ref[r, j] for j in range(blocks_ref.shape[1])]
        high = [high_ref[p] for p in picked]
        low = [low_ref[p] for p in picked]
        block = [halves(blocks_ref[r, j]) for j in range(blocks_ref.shape[1])]
        left = jnp.concatenate(high + high + low, axis=1)
        right = jnp.concatenate(
            [h for h, _ in block] + [l for _, l in block] + [h for h, _ in block], axis=1
        )
        result = lax.dot_general(
            left, right, (((1,), (1,)), ((), ())), preferred_element_type=F32
        )
        for y in range(gy_size):
            for v in range(out_ref.shape[1] // GROUP):
                packed = jnp.zeros((GROUP, cols), F32)
                for s in range(min(slots, 3 * groups - v * slots)):
                    q = v * slots + s
                    piece = result[q * GROUP : (q + 1) * GROUP]
                    if s != y:
                        piece = pltpu.roll(piece, ((s - y) * width) % cols, 1)
                    packed = jnp.where(owner == s, piece, packed)
                out_ref[y * tiles + r, v * GROUP : (v + 1) * GROUP, :] = packed


def zonal(pattern, blocks, field, gy_size, after):
    tiles, height, cols = field.shape
    width = cols // gy_size
    slots = LANES // width
    lines = -(-(height // GROUP) // slots) * GROUP

    def kernel(pattern_ref, blocks_ref, field_ref, after_ref, *refs):
        zonal_kernel(gy_size, pattern_ref, blocks_ref, field_ref, *refs)

    return pl.pallas_call(
        kernel,
        out_shape=struct(gy_size * tiles, lines, cols),
        in_specs=[smem(), whole(), whole(), anywhere()],
        out_specs=whole(),
        scratch_shapes=[pltpu.VMEM((tiles, height, cols), BF16)] * 2,
        compiler_params=params(),
        cost_estimate=cost(2.0),
        name="zonal",
    )(pattern, blocks, field, after)


def meridional_kernel(
    gx_size, gy_size, pattern_ref, blocks_ref, field_ref, out_ref, high_ref, low_ref
):
    devices, lines, cols = field_ref.shape
    tiles, block, _ = high_ref.shape
    rows = tiles * block // gy_size
    chunk = rows // gx_size
    width = cols // gy_size
    slots = LANES // width
    groups = chunk // GROUP
    owner = lane_ids((GROUP, cols)) // width
    for d in range(devices):
        pieces = []
        for g in range(groups):
            packed = jnp.zeros((GROUP, cols), F32)
            for c in range(3):
                q = c * groups + g
                v, s = divmod(q, slots)
                piece = field_ref[d, v * GROUP : (v + 1) * GROUP, :]
                if s != c:
                    piece = pltpu.roll(piece, ((c - s) * width) % cols, 1)
                packed = jnp.where(owner == c, piece, packed)
            pieces.append(packed)
        tile, line = divmod(d * chunk, block)
        high, low = halves(jnp.concatenate(pieces, axis=0))
        high_ref[tile, line : line + chunk, :] = high
        low_ref[tile, line : line + chunk, :] = low
    for r in range(blocks_ref.shape[0]):
        picked = [pattern_ref[r, j] for j in range(blocks_ref.shape[1])]
        high = [high_ref[p] for p in picked]
        low = [low_ref[p] for p in picked]
        parts = [halves(blocks_ref[r, j]) for j in range(blocks_ref.shape[1])]
        left = jnp.concatenate(
            [h for h, _ in parts] + [l for _, l in parts] + [h for h, _ in parts], axis=1
        )
        right = jnp.concatenate(high + high + low, axis=0)
        result = jnp.dot(left, right, preferred_element_type=F32)
        dest, line = divmod(r * block, rows)
        first = line // GROUP
        for c in range(3):
            for v in range(block // GROUP // slots):
                packed = jnp.zeros((GROUP, cols), F32)
                for s in range(slots):
                    g = v * slots + s
                    piece = result[g * GROUP : (g + 1) * GROUP]
                    if s != c:
                        piece = pltpu.roll(piece, ((s - c) * width) % cols, 1)
                    packed = jnp.where(owner == s, piece, packed)
                at = (c * (rows // GROUP) + first) // slots + v
                out_ref[dest, at * GROUP : (at + 1) * GROUP, :] = packed


def meridional(pattern, blocks, field, gx_size, gy_size, after):
    devices, lines, cols = field.shape
    tiles, _, block, _ = blocks.shape
    rows = tiles * block // gy_size
    slots = LANES // (cols // gy_size)

    def kernel(pattern_ref, blocks_ref, field_ref, after_ref, *refs):
        meridional_kernel(gx_size, gy_size, pattern_ref, blocks_ref, field_ref, *refs)

    return pl.pallas_call(
        kernel,
        out_shape=struct(gy_size, 3 * rows // slots, cols),
        in_specs=[smem(), whole(), whole(), anywhere()],
        out_specs=whole(),
        scratch_shapes=[pltpu.VMEM((tiles, block, cols), BF16)] * 2,
        compiler_params=params(),
        cost_estimate=cost(2.0),
        name="meridional",
    )(pattern, blocks, field, after)


def finish_kernel(field_ref, out_ref):
    sources, _, cols = field_ref.shape
    _, rows, _ = out_ref.shape
    width = cols // sources
    slots = LANES // width
    owner = lane_ids((GROUP, cols)) // width
    for c in range(3):
        for g in range(rows // GROUP):
            v, s = divmod(c * (rows // GROUP) + g, slots)
            packed = jnp.zeros((GROUP, cols), F32)
            for y in range(sources):
                piece = field_ref[y, v * GROUP : (v + 1) * GROUP, :]
                if s != y:
                    piece = pltpu.roll(piece, ((y - s) * width) % cols, 1)
                packed = jnp.where(owner == y, piece, packed)
            out_ref[c, g * GROUP : (g + 1) * GROUP, :] = packed


def finish(field, rows):
    sources, _, cols = field.shape
    return pl.pallas_call(
        finish_kernel,
        out_shape=struct(3, rows, cols),
        in_specs=[whole()],
        out_specs=whole(),
        compiler_params=params(),
        cost_estimate=cost(1.0),
        name="finish",
    )(field)


def shards(cot_u, cot_v, cot_t, levels, mixing, pattern_x, blocks_x, pattern_y, blocks_y):
    depth, rows, cols = cot_u.shape
    nx, ny = (lax.axis_size("gx"), lax.axis_size("gy"))
    up_x = [(i, i + 1) for i in range(nx - 1)]
    down_x = [(j, i) for i, j in up_x]
    up_y = [(i, i + 1) for i in range(ny - 1)]
    down_y = [(j, i) for i, j in up_y]
    place = lambda y, x: x * ny + y
    to_se = [(place(j, i), place(j - 1, i + 1)) for j in range(1, ny) for i in range(nx - 1)]
    to_nw = [(j, i) for i, j in to_se]

    level_col, level_row = edges(levels)
    level_col = lax.ppermute(level_col, "gx", up_x)
    level_row = lax.ppermute(level_row, "gy", up_y)
    field, wet_c, wet_u, wet_v = surface(
        levels, level_col, level_row, cot_u, cot_v, cot_t, nx
    )
    cots = (cot_u, cot_v, cot_t)
    lines = lax.all_to_all(field, "gx", 0, 0)

    east, west, north, south, corner_e, corner_w = rims(
        wet_c, wet_u, wet_v, mixing, *cots, field
    )
    halo_w = lax.ppermute(east, "gx", up_x)
    halo_e = lax.ppermute(west, "gx", down_x)
    halo_s = lax.ppermute(north, "gy", up_y)
    halo_n = lax.ppermute(south, "gy", down_y)
    halo_nw = lax.ppermute(corner_e, ("gx", "gy"), to_se)
    halo_se = lax.ppermute(corner_w, ("gx", "gy"), to_nw)

    packed = zonal(pattern_x, blocks_x, lines, ny, corner_e)
    columns = lax.all_to_all(packed, ("gy", "gx"), 0, 0)
    grads = adjoint(
        (wet_c, wet_u, wet_v, mixing),
        (halo_w, halo_e, halo_n, halo_s, halo_nw, halo_se),
        cots,
        packed,
        rows * ny,
    )
    sent = meridional(pattern_y, blocks_y, columns, nx, ny, grads[0])
    mixed = finish(lax.all_to_all(sent, "gy", 0, 0), rows)
    return (*grads, mixed)


def solution(mesh):
    grid = P(None, "gy", "gx")
    flat = P("gy", "gx")
    return jax.shard_map(
        shards,
        mesh=mesh,
        in_specs=(grid, grid, grid, flat, flat, P(), P(), P(), P()),
        out_specs=(grid, grid, grid, grid),
        check_vma=False,
    )
```

```python
import functools

import jax
import jax.numpy as jnp
from jax import lax
from jax.experimental import pallas as pl
from jax.experimental.pallas import tpu as pltpu
from jax.sharding import PartitionSpec as P

time_step = 0.5
gravity_scale = 0.05
coriolis_base = 0.4
zonal_slope = 0.3
north_slope = 0.2

LANES = 128
GROUP = 8
F32 = jnp.float32
BF16 = jnp.bfloat16
MIB = 1024 * 1024
BAND = 32


def whole():
    return pl.BlockSpec(memory_space=pltpu.VMEM)


def anywhere():
    return pl.BlockSpec(memory_space=pl.ANY)


def full(*shape):
    return pl.BlockSpec(shape, lambda i: (0,) * len(shape))


def smem():
    return pl.BlockSpec(memory_space=pltpu.SMEM)


def struct(*shape):
    return jax.ShapeDtypeStruct(shape, F32)


def params(mib):
    return pltpu.CompilerParams(vmem_limit_bytes=mib * MIB)


def cost(microseconds):
    return pl.CostEstimate(
        flops=int(microseconds * 1e6), bytes_accessed=int(microseconds * 3.0e6), transcendentals=0
    )


def has_before(axis):
    return lax.axis_index(axis) > 0


def has_after(axis):
    return lax.axis_index(axis) < lax.axis_size(axis) - 1


def lane_ids(shape):
    return lax.broadcasted_iota(jnp.int32, shape, 1)


def row_ids(shape):
    return lax.broadcasted_iota(jnp.int32, shape, 0)


def rim_kernel(
    step,
    levels_ref,
    mix_ref,
    u_ref,
    v_ref,
    t_ref,
    first_u_ref,
    first_v_ref,
    first_t_ref,
    last_u_ref,
    last_v_ref,
    last_t_ref,
    col_ref,
    row_ref,
    east_ref,
    west_ref,
    north_ref,
    south_ref,
):
    at = pl.program_id(0)
    rows, cols = mix_ref.shape
    depth = first_u_ref.shape[0]
    first = at * step
    chunk = 2 * GROUP
    lane = lane_ids((chunk, cols))
    edge = (lane == 0) | (lane == cols - 1)

    @pl.when(at == 0)
    def _():
        field = levels_ref[...].astype(F32)
        col_ref[...] = jnp.transpose(field)[cols - GROUP :]
        row_ref[...] = field[rows - GROUP :]
        east_ref[...] = jnp.zeros((rows, cols), F32)
        west_ref[...] = jnp.zeros((rows, cols), F32)
        mix = mix_ref[...]
        rest = north_ref.shape[0] - 3 * BAND
        north_ref[3 * BAND :, :] = jnp.broadcast_to(mix[rows - 1 :], (rest, cols))
        south_ref[3 * BAND :, :] = jnp.broadcast_to(mix[:1], (rest, cols))
        empty = jnp.zeros((BAND - depth, cols), F32)
        for f, ref in enumerate((last_u_ref, last_v_ref, last_t_ref)):
            line = ref[:, GROUP - 1 :, :].reshape(depth, cols)
            north_ref[f * BAND : (f + 1) * BAND, :] = jnp.concatenate([line, empty], axis=0)
        for f, ref in enumerate((first_u_ref, first_v_ref, first_t_ref)):
            line = ref[:, :1, :].reshape(depth, cols)
            south_ref[f * BAND : (f + 1) * BAND, :] = jnp.concatenate([line, empty], axis=0)

    flip = lax.rem(first, 2) == 1

    def body(i, carry):
        base = pl.multiple_of(i * chunk, chunk)
        here = pl.ds(base, chunk)
        sums = [None, None]
        for k in range(step):
            for f, ref in enumerate((u_ref, v_ref, t_ref)):
                value = jnp.where(edge, ref[k, here, :], 0.0)
                rolled = pltpu.roll(value, BAND * f + first + k + 1, 1)
                sums[k % 2] = rolled if sums[k % 2] is None else sums[k % 2] + rolled
        east_ref[here, :] += jnp.where(flip, sums[1], sums[0])
        west_ref[here, :] += jnp.where(flip, sums[0], sums[1])
        return carry

    lax.fori_loop(0, rows // chunk, body, 0, unroll=8)

    @pl.when(at == pl.num_programs(0) - 1)
    def _():
        ids = lane_ids((rows, cols))
        even = lax.rem(ids, 2) == 0
        mix = pltpu.roll(mix_ref[...], 3 * BAND + 1, 1)
        even_levels = east_ref[...]
        odd_levels = west_ref[...]
        east = jnp.where(even, even_levels, odd_levels)
        west = jnp.where(even, odd_levels, even_levels)
        east_ref[...] = jnp.where(ids == 3 * BAND, mix, east)
        west_ref[...] = jnp.where(ids == 3 * BAND + 1, mix, west)


def rims(levels, mixing, cots):
    depth, rows, cols = cots[0].shape
    step = 5
    lines = 3 * BAND + GROUP
    plane = full(rows, cols)
    block = pl.BlockSpec((step, rows, cols), lambda i: (i, 0, 0))
    top = rows // GROUP - 1
    first = pl.BlockSpec((depth, GROUP, cols), lambda i: (0, 0, 0))
    last = pl.BlockSpec((depth, GROUP, cols), lambda i: (0, top, 0))
    return pl.pallas_call(
        functools.partial(rim_kernel, step),
        grid=(depth // step,),
        out_shape=(struct(GROUP, rows), struct(GROUP, cols))
        + (struct(rows, cols),) * 2
        + (struct(lines, cols),) * 2,
        in_specs=[plane] * 2 + [block] * 3 + [first] * 3 + [last] * 3,
        out_specs=(full(GROUP, rows), full(GROUP, cols))
        + (plane,) * 2
        + (full(lines, cols),) * 2,
        compiler_params=params(12),
        cost_estimate=cost(6.0),
        name="rims",
    )(levels, mixing, *cots, *cots, *cots)


def surface_kernel(
    levels_ref,
    col_ref,
    row_ref,
    east_ref,
    west_ref,
    north_ref,
    south_ref,
    u_ref,
    v_ref,
    t_ref,
    out_ref,
    wet_c_ref,
    wet_u_ref,
    wet_v_ref,
    east_out_ref,
    west_out_ref,
    north_out_ref,
    south_out_ref,
):
    rows, cols = levels_ref.shape
    field = levels_ref[...].astype(F32)
    lane = lane_ids(field.shape)
    row = row_ids(field.shape)
    col = jnp.broadcast_to(jnp.transpose(col_ref[...])[:, GROUP - 1 :], field.shape)
    col = jnp.where(has_before("gx"), col, 0.0)
    west = jnp.where(lane == 0, col, pltpu.roll(field, 1, 1))
    line = jnp.broadcast_to(row_ref[GROUP - 1 :, :], field.shape)
    line = jnp.where(has_before("gy"), line, 0.0)
    south = jnp.where(row == 0, line, pltpu.roll(field, 1, 0))
    wet_u = jnp.minimum(field, west)
    wet_v = jnp.minimum(field, south)
    wets = (wet_u, wet_v, field)
    wet_c_ref[...] = field
    wet_u_ref[...] = wet_u
    wet_v_ref[...] = wet_v
    parts, chunk = (out_ref.shape[0], out_ref.shape[1] // 3)
    for comp, ref in enumerate((u_ref, v_ref, t_ref)):
        grad = jnp.where(wets[comp] > 0.0, time_step * ref[0], 0.0)
        for part in range(parts):
            out_ref[part, comp * chunk : (comp + 1) * chunk, :] = grad[
                part * chunk : (part + 1) * chunk
            ]
    for ref, out, place, shift in (
        (east_ref, east_out_ref, cols - 1, 0),
        (west_ref, west_out_ref, 0, 1),
    ):
        at = lax.rem(lane + cols - shift, cols)
        band = at // BAND
        level = lax.rem(at, BAND).astype(F32)
        limit = [jnp.broadcast_to(wet[:, place : place + 1], field.shape) for wet in wets]
        limit = jnp.where(band == 0, limit[0], jnp.where(band == 1, limit[1], limit[2]))
        out[...] = jnp.where((level < limit) | (band == 3), ref[...], 0.0)
    level = row_ids((BAND, cols)).astype(F32)
    for ref, out, place in ((north_ref, north_out_ref, rows - 1), (south_ref, south_out_ref, 0)):
        out[3 * BAND :, :] = ref[3 * BAND :, :]
        for f in range(3):
            band = slice(f * BAND, (f + 1) * BAND)
            out[band, :] = jnp.where(level < wets[f][place : place + 1], ref[band, :], 0.0)


def surface(levels, col, row, packed, cots, parts):
    rows, cols = levels.shape
    top = pl.BlockSpec((1, rows, cols), lambda i: (0, 0, 0))
    out = (parts, 3 * rows // parts, cols)
    rim = tuple(value.shape for value in packed)
    return pl.pallas_call(
        surface_kernel,
        grid=(1,),
        out_shape=(struct(*out),)
        + (struct(rows, cols),) * 3
        + tuple(struct(*shape) for shape in rim),
        in_specs=[full(rows, cols), full(GROUP, rows), full(GROUP, cols)]
        + [full(*shape) for shape in rim]
        + [top] * 3,
        out_specs=(full(*out),)
        + (full(rows, cols),) * 3
        + tuple(full(*shape) for shape in rim),
        compiler_params=params(12),
        cost_estimate=cost(2.0),
        name="surface",
    )(levels, col, row, *packed, *cots)


def corner_kernel(east_ref, west_ref, north_ref, south_ref, east_out_ref, west_out_ref):
    rows, cols = east_ref.shape
    north = jnp.where(has_after("gy"), north_ref[...], 0.0)
    south = jnp.where(has_before("gy"), south_ref[...], 0.0)
    missing = jnp.zeros((cols - north_ref.shape[0], cols), F32)
    corner_n = jnp.transpose(jnp.concatenate([north, missing], axis=0))[cols - 1 :]
    corner_s = jnp.transpose(jnp.concatenate([south, missing], axis=0))[:1]
    east_out_ref[:rows, :] = east_ref[...]
    west_out_ref[:rows, :] = west_ref[...]
    east_out_ref[rows:, :] = jnp.broadcast_to(corner_n, (GROUP, cols))
    west_out_ref[rows:, :] = jnp.broadcast_to(pltpu.roll(corner_s, 1, 1), (GROUP, cols))


def corners(east, west, halo_n, halo_s):
    rows, cols = east.shape
    return pl.pallas_call(
        corner_kernel,
        out_shape=(struct(rows + GROUP, cols),) * 2,
        in_specs=[whole()] * 4,
        out_specs=(whole(),) * 2,
        compiler_params=params(16),
        cost_estimate=cost(0.5),
        name="corners",
    )(east, west, halo_n, halo_s)


def adjoint_kernel(
    step,
    done,
    depth,
    total_rows,
    wet_c_ref,
    wet_u_ref,
    wet_v_ref,
    mix_ref,
    hw_ref,
    he_ref,
    hn_ref,
    hs_ref,
    old_refs,
    u_ref,
    v_ref,
    t_ref,
    gu_ref,
    gv_ref,
    gt_ref,
    state_ref,
    mix_n_ref,
    mix_s_ref,
    keep_ref,
    cor_ref,
    a_ref,
    b_ref,
    c_ref,
):
    rows, cols = mix_ref.shape
    at = pl.program_id(0)
    half = depth // 2
    first = depth - (done + at + 1) * step
    pad = GROUP
    cor_step = 0.25 * time_step * coriolis_base / total_rows
    slope_u = 0.5 * time_step * zonal_slope
    slope_v = 0.5 * time_step * north_slope
    weight = time_step * gravity_scale
    before_y, after_y = (has_before("gy"), has_after("gy"))

    @pl.when(at == 0)
    def _():
        shape = (rows, cols)
        lane = lane_ids(shape)
        row = row_ids(shape)
        start = lax.axis_index("gy") * rows
        lines = (row + start).astype(F32)
        cor = (0.25 * time_step * coriolis_base) * (0.5 + (lines + 0.5) / total_rows)
        cor_n = (0.25 * time_step * coriolis_base) * (0.5 + (lines + 1.5) / total_rows)
        cor_s = (0.25 * time_step * coriolis_base) * (0.5 + (lines - 0.5) / total_rows)
        cor_ref[...] = cor
        mix = mix_ref[...]
        keep_ref[...] = 1.0 - 4.0 * mix
        mix_n_ref[...] = jnp.where(
            row == rows - 1,
            jnp.broadcast_to(jnp.where(after_y, hn_ref[3 * BAND : 3 * BAND + 1, :], 0.0), shape),
            pltpu.roll(mix, rows - 1, 0),
        )
        mix_s_ref[...] = jnp.where(
            row == 0,
            jnp.broadcast_to(jnp.where(before_y, hs_ref[3 * BAND : 3 * BAND + 1, :], 0.0), shape),
            pltpu.roll(mix, 1, 0),
        )
        if old_refs:
            state_ref[...] = old_refs[0][...]
            return
        columns = jnp.where(has_after("gx"), he_ref[...], 0.0)
        east = columns[:rows]
        kind = lax.rem(lane + cols - 1, cols) // BAND
        mixed = east * jnp.broadcast_to(east[:, 3 * BAND + 1 : 3 * BAND + 2], shape)
        below = jnp.where(
            row == 0,
            jnp.broadcast_to(columns[rows : rows + 1], shape),
            pltpu.roll(east, 1, 0),
        )
        turned = cor * east + cor_s * below
        total = jnp.where(kind == 0, east, 0.0)
        reach = 1
        while reach < depth:
            total = total + pltpu.roll(total, cols - reach, 1)
            reach *= 2
        from_e = (
            mixed
            + jnp.where(kind == 1, pltpu.roll(turned, BAND, 1), 0.0)
            + jnp.where(kind == 2, pltpu.roll(weight * total, 2 * BAND, 1), 0.0)
        )
        columns = jnp.where(has_before("gx"), hw_ref[...], 0.0)
        west = columns[:rows]
        kind = lane // BAND
        mixed = west * jnp.broadcast_to(west[:, 3 * BAND : 3 * BAND + 1], shape)
        above = jnp.where(
            row == rows - 1,
            jnp.broadcast_to(columns[rows : rows + 1], shape),
            pltpu.roll(west, rows - 1, 0),
        )
        turned = cor * west + cor_n * above
        from_w = mixed - jnp.where(
            kind == 0,
            pltpu.roll(turned, cols - BAND, 1) + pltpu.roll(slope_u * west, cols - 2 * BAND, 1),
            0.0,
        )
        both = jnp.concatenate([from_e, from_w], axis=1)
        source = row_ids((2 * cols, 2 * cols))
        place = lane_ids((2 * cols, 2 * cols))
        part = place // cols
        spot = lax.rem(place, cols)
        pair = spot // 2
        slot = BAND * (pair // half) + part * half + lax.rem(pair, half)
        wanted = jnp.where(lax.rem(spot, 2) == 0, slot + 1, slot + cols)
        moves = jnp.where((source == wanted) & (pair < 3 * half), 1.0, 0.0).astype(BF16)
        moved = jnp.zeros((rows, 2 * cols), F32)
        for _ in range(3):
            high = both.astype(BF16)
            both = both - high.astype(F32)
            moved = moved + jnp.dot(high, moves, preferred_element_type=F32)
        state_ref[0] = moved[:, :cols]
        state_ref[1] = moved[:, cols:]
        state_ref[2] = jnp.zeros(shape, F32)
        state_ref[3] = jnp.zeros(shape, F32)

    fields = (
        (u_ref, wet_u_ref, a_ref),
        (v_ref, wet_v_ref, b_ref),
        (t_ref, wet_c_ref, c_ref),
    )

    def mask(i, carry):
        base = pl.multiple_of(i * 2 * GROUP, 2 * GROUP)
        here = pl.ds(base, 2 * GROUP)
        there = pl.ds(pl.multiple_of(base + pad, GROUP), 2 * GROUP)
        wets = [wet[here, :] for _, wet, _ in fields]
        for k in range(step):
            level = (first + k).astype(F32)
            for f, (ref, _, out) in enumerate(fields):
                out[k, there, :] = jnp.where(level < wets[f], ref[k, here, :], 0.0)
        return carry

    lax.fori_loop(0, rows // (2 * GROUP), mask, 0, unroll=8)
    for k in range(step):
        for f, (_, _, out) in enumerate(fields):
            slot = BAND * f + first + k
            out[k, pad - 1 : pad, :] = jnp.where(before_y, hs_ref[pl.ds(slot, 1), :], 0.0)
            out[k, pad + rows : pad + rows + 1, :] = jnp.where(
                after_y, hn_ref[pl.ds(slot, 1), :], 0.0
            )

    chunk = 2 * GROUP
    lane = lane_ids((chunk, cols))
    is_east = lane == cols - 1
    is_west = lane == 0
    part = (first >= half).astype(jnp.int32)

    def body(i, carry):
        base = pl.multiple_of(i * chunk, chunk)
        here = pl.ds(base, chunk)
        center = pl.ds(base + pad, chunk)
        north = pl.ds(base + pad + 1, chunk)
        south = pl.ds(base + pad - 1, chunk)
        mix = mix_ref[here, :]
        mix_n = mix_n_ref[here, :]
        mix_s = mix_s_ref[here, :]
        keep = keep_ref[here, :]
        cor = cor_ref[here, :]
        cor_n = cor + cor_step
        cor_s = cor - cor_step
        edges = state_ref[part, here, :]
        sum_a = state_ref[2, here, :]
        sum_d = state_ref[3, here, :]
        for k in reversed(range(step)):
            inner = first + k - part * half

            def both_sides(west, east, f, inner=inner):
                edge = pltpu.roll(edges, 2 * cols - 1 - 2 * (f * half + inner), 1)
                return jnp.where(is_west, edge, pltpu.roll(west, 1, 1)) + jnp.where(
                    is_east, edge, pltpu.roll(east, cols - 1, 1)
                )

            a = a_ref[k, center, :]
            a_n = a_ref[k, north, :]
            a_s = a_ref[k, south, :]
            b = b_ref[k, center, :]
            b_n = b_ref[k, north, :]
            b_s = b_ref[k, south, :]
            c = c_ref[k, center, :]
            c_n = c_ref[k, north, :]
            c_s = c_ref[k, south, :]
            mix_a = mix * a
            turn_b = cor * b + cor_n * b_n + slope_u * c
            gu_ref[k, here, :] = (
                keep * a
                + (mix_n * a_n + mix_s * a_s)
                - turn_b
                + both_sides(mix_a - turn_b, mix_a, 0)
            )
            mix_b = mix * b
            turn_a = cor * a + cor_s * a_s
            gv_ref[k, here, :] = (
                keep * b
                + (mix_n * b_n + mix_s * b_s)
                + (turn_a - slope_v * (c + c_s))
                + both_sides(mix_b, mix_b + turn_a, 1)
            )
            mix_c = mix * c
            sum_a = sum_a + weight * a
            sum_d = sum_d + weight * (b - b_n)
            gt_ref[k, here, :] = (
                keep * c
                + (mix_n * c_n + mix_s * c_s)
                - (sum_a + sum_d)
                + both_sides(mix_c, mix_c + sum_a, 2)
            )
        state_ref[2, here, :] = sum_a
        state_ref[3, here, :] = sum_d
        return carry

    lax.fori_loop(0, rows // chunk, body, 0, unroll=rows // chunk)


def adjoint(planes, halos, cots, after, total_rows, earlier=None):
    depth, rows, cols = cots[0].shape
    step = 5
    first = 2 * depth // (3 * step)
    done, steps = (0, first) if earlier is None else (first, depth // step - first)
    plane = full(rows, cols)
    top = depth // step - 1 - done
    block = pl.BlockSpec((step, rows, cols), lambda i: (top - i, 0, 0))
    grads, state = ((), ()) if earlier is None else earlier
    n_planes = len(planes) + len(halos)
    n_state = len(state)
    kept = (4, rows, cols)

    def kernel(*refs):
        front, refs = refs[:n_planes], refs[n_planes:]
        old, refs = refs[:n_state], refs[n_state:]
        ins, refs = refs[:3], refs[3 + 1 + len(grads) :]
        adjoint_kernel(step, done, depth, total_rows, *front, old, *ins, *refs)

    padded = pltpu.VMEM((step, rows + 2 * GROUP, cols), F32)
    aliases = {n_planes + n_state + 4 + i: i for i in range(len(grads))}
    result = pl.pallas_call(
        kernel,
        grid=(steps,),
        out_shape=(struct(depth, rows, cols),) * 3 + (struct(*kept),),
        in_specs=[plane] * len(planes)
        + [full(*halo.shape) for halo in halos]
        + [full(*kept)] * n_state
        + [block] * 3
        + [anywhere()] * (1 + len(grads)),
        out_specs=(block,) * 3 + (full(*kept),),
        scratch_shapes=[pltpu.VMEM((rows, cols), F32)] * 4 + [padded] * 3,
        input_output_aliases=aliases,
        compiler_params=params(20),
        cost_estimate=cost(3.0 * steps),
        name="adjoint",
    )(*planes, *halos, *state, *cots, after, *grads)
    return result[:3], result[3:]


def halves(value):
    high = value.astype(BF16)
    return high, (value - high.astype(F32)).astype(BF16)


def zonal_kernel(
    gy_size,
    pattern_ref,
    blocks_ref,
    field_ref,
    out_ref,
    high_ref,
    low_ref,
):
    tiles, height, cols = field_ref.shape
    chunk = height // 3
    width = cols // gy_size
    slots = LANES // width
    groups = chunk // GROUP
    owner = lane_ids((GROUP, cols)) // width
    for tile in range(tiles):
        high_ref[tile], low_ref[tile] = halves(field_ref[tile])
    for r in range(blocks_ref.shape[0]):
        picked = [pattern_ref[r, j] for j in range(blocks_ref.shape[1])]
        high = [high_ref[p] for p in picked]
        low = [low_ref[p] for p in picked]
        block = [halves(blocks_ref[r, j]) for j in range(blocks_ref.shape[1])]
        left = jnp.concatenate(high + high + low, axis=1)
        right = jnp.concatenate(
            [h for h, _ in block] + [l for _, l in block] + [h for h, _ in block], axis=1
        )
        result = lax.dot_general(
            left, right, (((1,), (1,)), ((), ())), preferred_element_type=F32
        )
        for y in range(gy_size):
            for v in range(out_ref.shape[1] // GROUP):
                packed = jnp.zeros((GROUP, cols), F32)
                for s in range(min(slots, 3 * groups - v * slots)):
                    q = v * slots + s
                    piece = result[q * GROUP : (q + 1) * GROUP]
                    if s != y:
                        piece = pltpu.roll(piece, ((s - y) * width) % cols, 1)
                    packed = jnp.where(owner == s, piece, packed)
                out_ref[y * tiles + r, v * GROUP : (v + 1) * GROUP, :] = packed


def zonal(pattern, blocks, field, gy_size):
    tiles, height, cols = field.shape
    width = cols // gy_size
    slots = LANES // width
    lines = -(-(height // GROUP) // slots) * GROUP

    return pl.pallas_call(
        functools.partial(zonal_kernel, gy_size),
        out_shape=struct(gy_size * tiles, lines, cols),
        in_specs=[smem()] + [whole()] * 2,
        out_specs=whole(),
        scratch_shapes=[pltpu.VMEM((tiles, height, cols), BF16)] * 2,
        compiler_params=params(16),
        cost_estimate=cost(2.0),
        name="zonal",
    )(pattern, blocks, field)


def meridional_kernel(
    gx_size, gy_size, pattern_ref, blocks_ref, field_ref, out_ref, high_ref, low_ref
):
    devices, lines, cols = field_ref.shape
    tiles, block, _ = high_ref.shape
    rows = tiles * block // gy_size
    chunk = rows // gx_size
    width = cols // gy_size
    slots = LANES // width
    groups = chunk // GROUP
    owner = lane_ids((GROUP, cols)) // width
    for d in range(devices):
        pieces = []
        for g in range(groups):
            packed = jnp.zeros((GROUP, cols), F32)
            for c in range(3):
                q = c * groups + g
                v, s = divmod(q, slots)
                piece = field_ref[d, v * GROUP : (v + 1) * GROUP, :]
                if s != c:
                    piece = pltpu.roll(piece, ((c - s) * width) % cols, 1)
                packed = jnp.where(owner == c, piece, packed)
            pieces.append(packed)
        tile, line = divmod(d * chunk, block)
        high, low = halves(jnp.concatenate(pieces, axis=0))
        high_ref[tile, line : line + chunk, :] = high
        low_ref[tile, line : line + chunk, :] = low
    for r in range(blocks_ref.shape[0]):
        picked = [pattern_ref[r, j] for j in range(blocks_ref.shape[1])]
        high = [high_ref[p] for p in picked]
        low = [low_ref[p] for p in picked]
        parts = [halves(blocks_ref[r, j]) for j in range(blocks_ref.shape[1])]
        left = jnp.concatenate(
            [h for h, _ in parts] + [l for _, l in parts] + [h for h, _ in parts], axis=1
        )
        right = jnp.concatenate(high + high + low, axis=0)
        result = jnp.dot(left, right, preferred_element_type=F32)
        dest, line = divmod(r * block, rows)
        first = line // GROUP
        for c in range(3):
            for v in range(block // GROUP // slots):
                packed = jnp.zeros((GROUP, cols), F32)
                for s in range(slots):
                    g = v * slots + s
                    piece = result[g * GROUP : (g + 1) * GROUP]
                    if s != c:
                        piece = pltpu.roll(piece, ((s - c) * width) % cols, 1)
                    packed = jnp.where(owner == s, piece, packed)
                at = (c * (rows // GROUP) + first) // slots + v
                out_ref[dest, at * GROUP : (at + 1) * GROUP, :] = packed


def meridional(pattern, blocks, field, gx_size, gy_size, after):
    devices, lines, cols = field.shape
    tiles, _, block, _ = blocks.shape
    rows = tiles * block // gy_size
    slots = LANES // (cols // gy_size)

    def kernel(pattern_ref, blocks_ref, field_ref, after_ref, *refs):
        meridional_kernel(gx_size, gy_size, pattern_ref, blocks_ref, field_ref, *refs)

    return pl.pallas_call(
        kernel,
        out_shape=struct(gy_size, 3 * rows // slots, cols),
        in_specs=[smem(), whole(), whole(), anywhere()],
        out_specs=whole(),
        scratch_shapes=[pltpu.VMEM((tiles, block, cols), BF16)] * 2,
        compiler_params=params(16),
        cost_estimate=cost(2.0),
        name="meridional",
    )(pattern, blocks, field, after)


def finish_kernel(field_ref, after_ref, out_ref):
    sources, _, cols = field_ref.shape
    _, rows, _ = out_ref.shape
    width = cols // sources
    slots = LANES // width
    owner = lane_ids((GROUP, cols)) // width
    for c in range(3):
        for g in range(rows // GROUP):
            v, s = divmod(c * (rows // GROUP) + g, slots)
            packed = jnp.zeros((GROUP, cols), F32)
            for y in range(sources):
                piece = field_ref[y, v * GROUP : (v + 1) * GROUP, :]
                if s != y:
                    piece = pltpu.roll(piece, ((y - s) * width) % cols, 1)
                packed = jnp.where(owner == y, piece, packed)
            out_ref[c, g * GROUP : (g + 1) * GROUP, :] = packed


def finish(field, rows, after):
    sources, _, cols = field.shape
    return pl.pallas_call(
        finish_kernel,
        out_shape=struct(3, rows, cols),
        in_specs=[whole(), anywhere()],
        out_specs=whole(),
        compiler_params=params(16),
        cost_estimate=cost(1.0),
        name="finish",
    )(field, after)


def shards(cot_u, cot_v, cot_t, levels, mixing, pattern_x, blocks_x, pattern_y, blocks_y):
    depth, rows, cols = cot_u.shape
    nx, ny = (lax.axis_size("gx"), lax.axis_size("gy"))
    up_x = [(i, (i + 1) % nx) for i in range(nx)]
    down_x = [(j, i) for i, j in up_x]
    up_y = [(i, (i + 1) % ny) for i in range(ny)]
    down_y = [(j, i) for i, j in up_y]

    cots = tuple(pltpu.with_memory_space_constraint(c, pltpu.HBM) for c in (cot_u, cot_v, cot_t))
    level_col, level_row, *packed = rims(levels, mixing, cots)
    level_col = lax.ppermute(level_col, "gx", up_x)
    level_row = lax.ppermute(level_row, "gy", up_y)
    field, wet_c, wet_u, wet_v, east, west, north, south = surface(
        levels, level_col, level_row, packed, cots, nx
    )
    lines = lax.all_to_all(field, "gx", 0, 0)
    halo_s = lax.ppermute(north, "gy", up_y)
    halo_n = lax.ppermute(south, "gy", down_y)
    east, west = corners(east, west, halo_n, halo_s)
    halo_w = lax.ppermute(east, "gx", up_x)
    halo_e = lax.ppermute(west, "gx", down_x)
    packed = zonal(pattern_x, blocks_x, lines, ny)
    packed, halo_w, halo_e = lax.optimization_barrier((packed, halo_w, halo_e))
    columns = lax.all_to_all(packed, ("gy", "gx"), 0, 0)
    planes = (wet_c, wet_u, wet_v, mixing)
    halos = (halo_w, halo_e, halo_n, halo_s)
    grads, state = adjoint(planes, halos, cots, packed, rows * ny)
    sent = meridional(pattern_y, blocks_y, columns, nx, ny, state[-1])
    back = lax.all_to_all(sent, "gy", 0, 0)
    grads = tuple(pltpu.with_memory_space_constraint(g, pltpu.HBM) for g in grads)
    grads, token = adjoint(planes, halos, cots, sent, rows * ny, (grads, state))
    mixed = finish(back, rows, token[0])
    return (*grads, mixed)


def solution(mesh):
    grid = P(None, "gy", "gx")
    flat = P("gy", "gx")
    return jax.shard_map(
        shards,
        mesh=mesh,
        in_specs=(grid, grid, grid, flat, flat, P(), P(), P(), P()),
        out_specs=(grid, grid, grid, grid),
        check_vma=False,
    )
```

```python
import functools

import jax
import jax.numpy as jnp
from jax import lax
from jax.experimental import pallas as pl
from jax.experimental.pallas import tpu as pltpu
from jax.sharding import PartitionSpec as P

time_step = 0.5
gravity_scale = 0.05
coriolis_base = 0.4
zonal_slope = 0.3
north_slope = 0.2

LANES = 128
GROUP = 8
F32 = jnp.float32
BF16 = jnp.bfloat16
MIB = 1024 * 1024
BAND = 32


def whole():
    return pl.BlockSpec(memory_space=pltpu.VMEM)


def anywhere():
    return pl.BlockSpec(memory_space=pl.ANY)


def full(*shape):
    return pl.BlockSpec(shape, lambda i: (0,) * len(shape))


def smem():
    return pl.BlockSpec(memory_space=pltpu.SMEM)


def struct(*shape):
    return jax.ShapeDtypeStruct(shape, F32)


def params(mib):
    return pltpu.CompilerParams(vmem_limit_bytes=mib * MIB)


def cost(microseconds):
    return pl.CostEstimate(
        flops=int(microseconds * 1e6), bytes_accessed=int(microseconds * 3.0e6), transcendentals=0
    )


def has_before(axis):
    return lax.axis_index(axis) > 0


def has_after(axis):
    return lax.axis_index(axis) < lax.axis_size(axis) - 1


def lane_ids(shape):
    return lax.broadcasted_iota(jnp.int32, shape, 1)


def row_ids(shape):
    return lax.broadcasted_iota(jnp.int32, shape, 0)


def edge_kernel(levels_ref, col_ref, row_ref):
    rows, cols = levels_ref.shape
    field = levels_ref[...].astype(F32)
    col_ref[...] = jnp.transpose(field)[cols - GROUP :]
    row_ref[...] = field[rows - GROUP :]


def edges(levels):
    rows, cols = levels.shape
    return pl.pallas_call(
        edge_kernel,
        grid=(1,),
        out_shape=(struct(GROUP, rows), struct(GROUP, cols)),
        in_specs=[full(rows, cols)],
        out_specs=(full(GROUP, rows), full(GROUP, cols)),
        compiler_params=params(4),
        cost_estimate=cost(1.0),
        name="edges",
    )(levels)


def rim_kernel(
    step,
    mix_ref,
    u_ref,
    v_ref,
    t_ref,
    east_ref,
    west_ref,
    north_ref,
    south_ref,
    top_ref,
    u_here,
    v_here,
    t_here,
    arrived,
):
    depth, rows, cols = u_ref.shape
    fields = ((u_ref, u_here), (v_ref, v_here), (t_ref, t_here))
    chunk = 2 * GROUP
    lane = lane_ids((chunk, cols))
    edge = (lane == 0) | (lane == cols - 1)

    def copy(f, at):
        levels = pl.ds(at * step, step)
        source, target = fields[f]
        return pltpu.make_async_copy(source.at[levels], target.at[levels], arrived.at[f, at])

    for at in range(depth // step):
        for f in range(3):
            copy(f, at).start()
    east_ref[...] = jnp.zeros((rows, cols), F32)
    west_ref[...] = jnp.zeros((rows, cols), F32)
    mix = mix_ref[...]
    rest = north_ref.shape[0] - 3 * BAND
    north_ref[3 * BAND :, :] = jnp.broadcast_to(mix[rows - 1 :], (rest, cols))
    south_ref[3 * BAND :, :] = jnp.broadcast_to(mix[:1], (rest, cols))

    def levels(at, carry):
        first = at * step
        flip = lax.rem(first, 2) == 1
        for f in range(3):
            copy(f, at).wait()

        def body(i, inner):
            here = pl.ds(pl.multiple_of(i * chunk, chunk), chunk)
            sums = [None, None]
            for k in range(step):
                for f in range(3):
                    value = jnp.where(edge, fields[f][1][first + k, here, :], 0.0)
                    moved = pltpu.roll(value, BAND * f + first + k + 1, 1)
                    sums[k % 2] = moved if sums[k % 2] is None else sums[k % 2] + moved
            east_ref[here, :] += jnp.where(flip, sums[1], sums[0])
            west_ref[here, :] += jnp.where(flip, sums[0], sums[1])
            return inner

        lax.fori_loop(0, rows // chunk, body, 0, unroll=8)
        return carry

    lax.fori_loop(0, depth // step, levels, 0)
    ids = lane_ids((rows, cols))
    even = lax.rem(ids, 2) == 0
    mix = pltpu.roll(mix, 3 * BAND + 1, 1)
    even_levels = east_ref[...]
    odd_levels = west_ref[...]
    east = jnp.where(even, even_levels, odd_levels)
    west = jnp.where(even, odd_levels, even_levels)
    east_ref[...] = jnp.where(ids == 3 * BAND, mix, east)
    west_ref[...] = jnp.where(ids == 3 * BAND + 1, mix, west)
    empty = jnp.zeros((BAND - depth, cols), F32)
    for f in range(3):
        band = slice(f * BAND, (f + 1) * BAND)
        here = fields[f][1]
        for out, place in ((north_ref, rows - 1), (south_ref, 0)):
            line = here[:, place : place + 1, :].reshape(depth, cols)
            out[band, :] = jnp.concatenate([line, empty], axis=0)
        top_ref[f] = here[0]


def rims(mixing, cots):
    depth, rows, cols = cots[0].shape
    step = 5
    lines = 3 * BAND + GROUP
    return pl.pallas_call(
        functools.partial(rim_kernel, step),
        out_shape=(struct(rows, cols),) * 2
        + (struct(lines, cols),) * 2
        + (struct(3, rows, cols),),
        in_specs=[whole()] + [anywhere()] * 3,
        out_specs=(whole(),) * 5,
        scratch_shapes=[pltpu.VMEM((depth, rows, cols), F32)] * 3
        + [pltpu.SemaphoreType.DMA((3, depth // step))],
        compiler_params=params(14),
        cost_estimate=cost(6.0),
        name="rims",
    )(mixing, *cots)


def surface_kernel(
    levels_ref,
    col_ref,
    row_ref,
    east_ref,
    west_ref,
    north_ref,
    south_ref,
    top_ref,
    out_ref,
    wet_c_ref,
    wet_u_ref,
    wet_v_ref,
    east_out_ref,
    west_out_ref,
    north_out_ref,
    south_out_ref,
):
    rows, cols = levels_ref.shape
    field = levels_ref[...].astype(F32)
    lane = lane_ids(field.shape)
    row = row_ids(field.shape)
    col = jnp.broadcast_to(jnp.transpose(col_ref[...])[:, GROUP - 1 :], field.shape)
    col = jnp.where(has_before("gx"), col, 0.0)
    west = jnp.where(lane == 0, col, pltpu.roll(field, 1, 1))
    line = jnp.broadcast_to(row_ref[GROUP - 1 :, :], field.shape)
    line = jnp.where(has_before("gy"), line, 0.0)
    south = jnp.where(row == 0, line, pltpu.roll(field, 1, 0))
    wet_u = jnp.minimum(field, west)
    wet_v = jnp.minimum(field, south)
    wets = (wet_u, wet_v, field)
    wet_c_ref[...] = field
    wet_u_ref[...] = wet_u
    wet_v_ref[...] = wet_v
    for comp in range(3):
        out_ref[comp] = jnp.where(wets[comp] > 0.0, time_step * top_ref[comp], 0.0)
    for ref, out, place, shift in (
        (east_ref, east_out_ref, cols - 1, 0),
        (west_ref, west_out_ref, 0, 1),
    ):
        at = lax.rem(lane + cols - shift, cols)
        band = at // BAND
        level = lax.rem(at, BAND).astype(F32)
        limit = [jnp.broadcast_to(wet[:, place : place + 1], field.shape) for wet in wets]
        limit = jnp.where(band == 0, limit[0], jnp.where(band == 1, limit[1], limit[2]))
        out[...] = jnp.where((level < limit) | (band == 3), ref[...], 0.0)
    level = row_ids((BAND, cols)).astype(F32)
    for ref, out, place in ((north_ref, north_out_ref, rows - 1), (south_ref, south_out_ref, 0)):
        out[3 * BAND :, :] = ref[3 * BAND :, :]
        for f in range(3):
            band = slice(f * BAND, (f + 1) * BAND)
            out[band, :] = jnp.where(level < wets[f][place : place + 1], ref[band, :], 0.0)


def surface(levels, col, row, packed):
    rows, cols = levels.shape
    rim = tuple(struct(*value.shape) for value in packed[:4])
    return pl.pallas_call(
        surface_kernel,
        out_shape=(struct(3, rows, cols),) + (struct(rows, cols),) * 3 + rim,
        in_specs=[whole()] * 8,
        out_specs=(whole(),) * 8,
        compiler_params=params(4),
        cost_estimate=cost(1.5),
        name="surface",
    )(levels, col, row, *packed)


def corner_kernel(north_ref, south_ref, east_ref, west_ref, north_out_ref, south_out_ref):
    spot = row_ids(north_ref.shape) == 3 * BAND + 1
    last = east_ref.shape[0] - 1
    corner = jnp.broadcast_to(east_ref[last:, :], north_ref.shape)
    north_out_ref[...] = jnp.where(spot, corner, north_ref[...])
    corner = jnp.broadcast_to(west_ref[:1, :], south_ref.shape)
    south_out_ref[...] = jnp.where(spot, corner, south_ref[...])


def corners(north, south, halo_e, halo_w):
    return pl.pallas_call(
        corner_kernel,
        out_shape=(struct(*north.shape),) * 2,
        in_specs=[whole()] * 4,
        out_specs=(whole(),) * 2,
        compiler_params=params(4),
        cost_estimate=cost(0.3),
        name="corners",
    )(north, south, halo_e, halo_w)


def adjoint_kernel(
    step,
    done,
    depth,
    total_rows,
    wet_c_ref,
    wet_u_ref,
    wet_v_ref,
    mix_ref,
    hw_ref,
    he_ref,
    hn_ref,
    hs_ref,
    old_refs,
    u_ref,
    v_ref,
    t_ref,
    gu_ref,
    gv_ref,
    gt_ref,
    state_ref,
    mix_n_ref,
    mix_s_ref,
    keep_ref,
    cor_ref,
    a_ref,
    b_ref,
    c_ref,
):
    rows, cols = mix_ref.shape
    at = pl.program_id(0)
    half = depth // 2
    first = depth - (done + at + 1) * step
    pad = GROUP
    cor_step = 0.25 * time_step * coriolis_base / total_rows
    slope_u = 0.5 * time_step * zonal_slope
    slope_v = 0.5 * time_step * north_slope
    weight = time_step * gravity_scale
    before_y, after_y = (has_before("gy"), has_after("gy"))

    @pl.when(at == 0)
    def _():
        shape = (rows, cols)
        lane = lane_ids(shape)
        row = row_ids(shape)
        start = lax.axis_index("gy") * rows
        lines = (row + start).astype(F32)
        cor = (0.25 * time_step * coriolis_base) * (0.5 + (lines + 0.5) / total_rows)
        cor_n = (0.25 * time_step * coriolis_base) * (0.5 + (lines + 1.5) / total_rows)
        cor_s = (0.25 * time_step * coriolis_base) * (0.5 + (lines - 0.5) / total_rows)
        cor_ref[...] = cor
        mix = mix_ref[...]
        keep_ref[...] = 1.0 - 4.0 * mix
        mix_n_ref[...] = jnp.where(
            row == rows - 1,
            jnp.broadcast_to(jnp.where(after_y, hn_ref[3 * BAND : 3 * BAND + 1, :], 0.0), shape),
            pltpu.roll(mix, rows - 1, 0),
        )
        mix_s_ref[...] = jnp.where(
            row == 0,
            jnp.broadcast_to(jnp.where(before_y, hs_ref[3 * BAND : 3 * BAND + 1, :], 0.0), shape),
            pltpu.roll(mix, 1, 0),
        )
        if old_refs:
            state_ref[...] = old_refs[0][...]
            return
        east = jnp.where(has_after("gx"), he_ref[...], 0.0)
        corner = hs_ref[3 * BAND + 1 : 3 * BAND + 2, :]
        corner = jnp.where(has_after("gx") & before_y, corner, 0.0)
        kind = lax.rem(lane + cols - 1, cols) // BAND
        mixed = east * jnp.broadcast_to(east[:, 3 * BAND + 1 : 3 * BAND + 2], shape)
        below = jnp.where(
            row == 0,
            jnp.broadcast_to(corner, shape),
            pltpu.roll(east, 1, 0),
        )
        turned = cor * east + cor_s * below
        total = jnp.where(kind == 0, east, 0.0)
        reach = 1
        while reach < depth:
            total = total + pltpu.roll(total, cols - reach, 1)
            reach *= 2
        from_e = (
            mixed
            + jnp.where(kind == 1, pltpu.roll(turned, BAND, 1), 0.0)
            + jnp.where(kind == 2, pltpu.roll(weight * total, 2 * BAND, 1), 0.0)
        )
        west = jnp.where(has_before("gx"), hw_ref[...], 0.0)
        corner = hn_ref[3 * BAND + 1 : 3 * BAND + 2, :]
        corner = jnp.where(has_before("gx") & after_y, corner, 0.0)
        kind = lane // BAND
        mixed = west * jnp.broadcast_to(west[:, 3 * BAND : 3 * BAND + 1], shape)
        above = jnp.where(
            row == rows - 1,
            jnp.broadcast_to(corner, shape),
            pltpu.roll(west, rows - 1, 0),
        )
        turned = cor * west + cor_n * above
        from_w = mixed - jnp.where(
            kind == 0,
            pltpu.roll(turned, cols - BAND, 1) + pltpu.roll(slope_u * west, cols - 2 * BAND, 1),
            0.0,
        )
        both = jnp.concatenate([from_e, from_w], axis=1)
        source = row_ids((2 * cols, 2 * cols))
        place = lane_ids((2 * cols, 2 * cols))
        part = place // cols
        spot = lax.rem(place, cols)
        pair = spot // 2
        slot = BAND * (pair // half) + part * half + lax.rem(pair, half)
        wanted = jnp.where(lax.rem(spot, 2) == 0, slot + 1, slot + cols)
        moves = jnp.where((source == wanted) & (pair < 3 * half), 1.0, 0.0).astype(BF16)
        moved = jnp.zeros((rows, 2 * cols), F32)
        for _ in range(3):
            high = both.astype(BF16)
            both = both - high.astype(F32)
            moved = moved + jnp.dot(high, moves, preferred_element_type=F32)
        state_ref[0] = moved[:, :cols]
        state_ref[1] = moved[:, cols:]
        state_ref[2] = jnp.zeros(shape, F32)
        state_ref[3] = jnp.zeros(shape, F32)

    fields = (
        (u_ref, wet_u_ref, a_ref),
        (v_ref, wet_v_ref, b_ref),
        (t_ref, wet_c_ref, c_ref),
    )

    def mask(i, carry):
        base = pl.multiple_of(i * 2 * GROUP, 2 * GROUP)
        here = pl.ds(base, 2 * GROUP)
        there = pl.ds(pl.multiple_of(base + pad, GROUP), 2 * GROUP)
        wets = [wet[here, :] for _, wet, _ in fields]
        for k in range(step):
            level = (first + k).astype(F32)
            for f, (ref, _, out) in enumerate(fields):
                out[k, there, :] = jnp.where(level < wets[f], ref[k, here, :], 0.0)
        return carry

    lax.fori_loop(0, rows // (2 * GROUP), mask, 0, unroll=8)
    for k in range(step):
        for f, (_, _, out) in enumerate(fields):
            slot = BAND * f + first + k
            out[k, pad - 1 : pad, :] = jnp.where(before_y, hs_ref[pl.ds(slot, 1), :], 0.0)
            out[k, pad + rows : pad + rows + 1, :] = jnp.where(
                after_y, hn_ref[pl.ds(slot, 1), :], 0.0
            )

    chunk = 2 * GROUP
    lane = lane_ids((chunk, cols))
    is_east = lane == cols - 1
    is_west = lane == 0
    part = (first >= half).astype(jnp.int32)

    def body(i, carry):
        base = pl.multiple_of(i * chunk, chunk)
        here = pl.ds(base, chunk)
        center = pl.ds(base + pad, chunk)
        north = pl.ds(base + pad + 1, chunk)
        south = pl.ds(base + pad - 1, chunk)
        mix = mix_ref[here, :]
        mix_n = mix_n_ref[here, :]
        mix_s = mix_s_ref[here, :]
        keep = keep_ref[here, :]
        cor = cor_ref[here, :]
        cor_n = cor + cor_step
        cor_s = cor - cor_step
        edges = state_ref[part, here, :]
        sum_a = state_ref[2, here, :]
        sum_d = state_ref[3, here, :]
        for k in reversed(range(step)):
            inner = first + k - part * half

            def both_sides(west, east, f, inner=inner):
                edge = pltpu.roll(edges, 2 * cols - 1 - 2 * (f * half + inner), 1)
                return jnp.where(is_west, edge, pltpu.roll(west, 1, 1)) + jnp.where(
                    is_east, edge, pltpu.roll(east, cols - 1, 1)
                )

            a = a_ref[k, center, :]
            a_n = a_ref[k, north, :]
            a_s = a_ref[k, south, :]
            b = b_ref[k, center, :]
            b_n = b_ref[k, north, :]
            b_s = b_ref[k, south, :]
            c = c_ref[k, center, :]
            c_n = c_ref[k, north, :]
            c_s = c_ref[k, south, :]
            mix_a = mix * a
            turn_b = cor * b + cor_n * b_n + slope_u * c
            gu_ref[k, here, :] = (
                keep * a
                + (mix_n * a_n + mix_s * a_s)
                - turn_b
                + both_sides(mix_a - turn_b, mix_a, 0)
            )
            mix_b = mix * b
            turn_a = cor * a + cor_s * a_s
            gv_ref[k, here, :] = (
                keep * b
                + (mix_n * b_n + mix_s * b_s)
                + (turn_a - slope_v * (c + c_s))
                + both_sides(mix_b, mix_b + turn_a, 1)
            )
            mix_c = mix * c
            sum_a = sum_a + weight * a
            sum_d = sum_d + weight * (b - b_n)
            gt_ref[k, here, :] = (
                keep * c
                + (mix_n * c_n + mix_s * c_s)
                - (sum_a + sum_d)
                + both_sides(mix_c, mix_c + sum_a, 2)
            )
        state_ref[2, here, :] = sum_a
        state_ref[3, here, :] = sum_d
        return carry

    lax.fori_loop(0, rows // chunk, body, 0, unroll=rows // chunk)


def adjoint(planes, halos, cots, after, total_rows, earlier=None):
    depth, rows, cols = cots[0].shape
    step = 5
    first = depth // (3 * step)
    done, steps = (0, first) if earlier is None else (first, depth // step - first)
    plane = full(rows, cols)
    top = depth // step - 1 - done
    block = pl.BlockSpec((step, rows, cols), lambda i: (top - i, 0, 0))
    grads, state = ((), ()) if earlier is None else earlier
    n_planes = len(planes) + len(halos)
    n_state = len(state)
    kept = (4, rows, cols)

    def kernel(*refs):
        front, refs = refs[:n_planes], refs[n_planes:]
        old, refs = refs[:n_state], refs[n_state:]
        ins, refs = refs[:3], refs[3 + 1 + len(grads) :]
        adjoint_kernel(step, done, depth, total_rows, *front, old, *ins, *refs)

    padded = pltpu.VMEM((step, rows + 2 * GROUP, cols), F32)
    aliases = {n_planes + n_state + 4 + i: i for i in range(len(grads))}
    result = pl.pallas_call(
        kernel,
        grid=(steps,),
        out_shape=(struct(depth, rows, cols),) * 3 + (struct(*kept),),
        in_specs=[plane] * len(planes)
        + [full(*halo.shape) for halo in halos]
        + [full(*kept)] * n_state
        + [block] * 3
        + [anywhere()] * (1 + len(grads)),
        out_specs=(block,) * 3 + (full(*kept),),
        scratch_shapes=[pltpu.VMEM((rows, cols), F32)] * 4 + [padded] * 3,
        input_output_aliases=aliases,
        compiler_params=params(16),
        cost_estimate=cost(3.0 * steps),
        name="adjoint",
    )(*planes, *halos, *state, *cots, after, *grads)
    return result[:3], result[3:]


def halves(value):
    high = value.astype(BF16)
    return high, (value - high.astype(F32)).astype(BF16)


def product(blocks, fields, field_first):
    high = [h for h, _ in blocks], [h for h, _ in fields]
    low = [l for _, l in blocks], [l for _, l in fields]
    left = jnp.concatenate(high[0] + low[0] + high[0], axis=1)
    if field_first:
        right = jnp.concatenate(high[1] + high[1] + low[1], axis=1)
        return lax.dot_general(
            right, left, (((1,), (1,)), ((), ())), preferred_element_type=F32
        )
    right = jnp.concatenate(high[1] + high[1] + low[1], axis=0)
    return jnp.dot(left, right, preferred_element_type=F32)


def zonal_kernel(pattern_ref, blocks_ref, field_ref, after_ref, out_ref, high_ref, low_ref):
    for tile in range(field_ref.shape[0]):
        high_ref[tile], low_ref[tile] = halves(field_ref[tile])
    for r in range(blocks_ref.shape[0]):
        entries = range(blocks_ref.shape[1])
        picked = [pattern_ref[r, j] for j in entries]
        out_ref[r] = product(
            [halves(blocks_ref[r, j]) for j in entries],
            [(high_ref[p], low_ref[p]) for p in picked],
            True,
        )


def zonal(pattern, blocks, field, after):
    return pl.pallas_call(
        zonal_kernel,
        out_shape=struct(*field.shape),
        in_specs=[smem()] + [whole()] * 2 + [anywhere()],
        out_specs=whole(),
        scratch_shapes=[pltpu.VMEM(field.shape, BF16)] * 2,
        compiler_params=params(6),
        cost_estimate=cost(2.0),
        name="zonal",
    )(pattern, blocks, field, after)


def meridional_kernel(pattern_ref, blocks_ref, field_refs, out_ref, high_ref, low_ref):
    _, block, _ = high_ref.shape
    _, rows, cols = field_refs[0].shape
    chunk = out_ref.shape[1] // 3
    mine = rows // block
    me = lax.axis_index("gy")
    for m, ref in enumerate(field_refs):
        first = (me ^ m) * mine
        for h in range(mine):
            here = slice(h * block, (h + 1) * block)
            value = jnp.concatenate([ref[c, here, :] for c in range(3)], axis=1)
            high_ref[first + h], low_ref[first + h] = halves(value)
    entries = range(blocks_ref.shape[1])
    for h in range(mine):
        r = me * mine + h
        picked = [pattern_ref[r, j] for j in entries]
        result = product(
            [halves(blocks_ref[r, j]) for j in entries],
            [(high_ref[p], low_ref[p]) for p in picked],
            False,
        )
        for line in range(0, block, chunk):
            part = (h * block + line) // chunk
            for c in range(3):
                out_ref[part, c * chunk : (c + 1) * chunk, :] = result[
                    line : line + chunk, c * cols : (c + 1) * cols
                ]


def meridional(pattern, blocks, fields, parts):
    n = len(fields)
    _, rows, cols = fields[0].shape
    tiles, _, block, _ = blocks.shape

    def kernel(pattern_ref, blocks_ref, *refs):
        meridional_kernel(pattern_ref, blocks_ref, refs[:n], *refs[n:])

    return pl.pallas_call(
        kernel,
        out_shape=struct(parts, 3 * rows // parts, cols),
        in_specs=[smem()] + [whole()] * (1 + n),
        out_specs=whole(),
        scratch_shapes=[pltpu.VMEM((tiles, block, 3 * cols), BF16)] * 2,
        compiler_params=params(4 + n),
        cost_estimate=cost(2.0),
        name="meridional",
    )(pattern, blocks, *fields)


def finish_kernel(field_ref, after_ref, out_ref):
    parts, height, cols = field_ref.shape
    chunk = height // 3
    for part in range(parts):
        for c in range(3):
            out_ref[c, part * chunk : (part + 1) * chunk, :] = field_ref[
                part, c * chunk : (c + 1) * chunk, :
            ]


def finish(field, after):
    parts, height, cols = field.shape
    return pl.pallas_call(
        finish_kernel,
        out_shape=struct(3, parts * height // 3, cols),
        in_specs=[whole(), anywhere()],
        out_specs=whole(),
        compiler_params=params(4),
        cost_estimate=cost(0.7),
        name="finish",
    )(field, after)


def shards(cot_u, cot_v, cot_t, levels, mixing, pattern_x, blocks_x, pattern_y, blocks_y):
    depth, rows, cols = cot_u.shape
    nx, ny = (lax.axis_size("gx"), lax.axis_size("gy"))
    up_x = [(i, (i + 1) % nx) for i in range(nx)]
    down_x = [(j, i) for i, j in up_x]
    up_y = [(i, (i + 1) % ny) for i in range(ny)]
    down_y = [(j, i) for i, j in up_y]

    mixing = pltpu.with_memory_space_constraint(mixing, pltpu.HBM)
    cots = tuple(pltpu.with_memory_space_constraint(c, pltpu.HBM) for c in (cot_u, cot_v, cot_t))
    level_col, level_row = edges(levels)
    level_col = lax.ppermute(level_col, "gx", up_x)
    level_row = lax.ppermute(level_row, "gy", up_y)
    packed = rims(mixing, cots)
    field, wet_c, wet_u, wet_v, east, west, north, south = surface(
        levels, level_col, level_row, packed
    )
    halo_w = lax.ppermute(east, "gx", up_x)
    halo_e = lax.ppermute(west, "gx", down_x)
    tiles = {0: field}
    bit = ny // 2
    while bit:
        tiles[bit] = lax.ppermute(field, "gy", [(i, i ^ bit) for i in range(ny)])
        bit //= 2
    own = [m for m in tiles if m]
    *received, halo_w, halo_e = lax.optimization_barrier(
        (*(tiles[m] for m in own), halo_w, halo_e)
    )
    tiles.update(zip(own, received))
    bit = ny // 4
    while bit:
        for m in sorted(m for m in tiles if m and m % (2 * bit) == 0):
            tiles[m ^ bit] = lax.ppermute(tiles[m], "gy", [(i, i ^ bit) for i in range(ny)])
        bit //= 2
    north, south = corners(north, south, halo_e, halo_w)
    halo_s = lax.ppermute(north, "gy", up_y)
    halo_n = lax.ppermute(south, "gy", down_y)
    mixed = meridional(pattern_y, blocks_y, [tiles[m] for m in range(ny)], nx)
    mixed, halo_s, halo_n = lax.optimization_barrier((mixed, halo_s, halo_n))
    lines = lax.all_to_all(mixed, "gx", 0, 0)
    planes = (wet_c, wet_u, wet_v, mixing)
    halos = (halo_w, halo_e, halo_n, halo_s)
    grads, state = adjoint(planes, halos, cots, mixed, rows * ny)
    turned = zonal(pattern_x, blocks_x, lines, state[0])
    back = lax.all_to_all(turned, "gx", 0, 0)
    grads = tuple(pltpu.with_memory_space_constraint(g, pltpu.HBM) for g in grads)
    grads, token = adjoint(planes, halos, cots, turned, rows * ny, (grads, state))
    return (*grads, finish(back, token[0]))


def solution(mesh):
    grid = P(None, "gy", "gx")
    flat = P("gy", "gx")
    return jax.shard_map(
        shards,
        mesh=mesh,
        in_specs=(grid, grid, grid, flat, flat, P(), P(), P(), P()),
        out_specs=(grid, grid, grid, grid),
        check_vma=False,
    )
```

```python
import functools

import jax
import jax.numpy as jnp
from jax import lax
from jax.experimental import pallas as pl
from jax.experimental.pallas import tpu as pltpu
from jax.sharding import PartitionSpec as P

time_step = 0.5
gravity_scale = 0.05
coriolis_base = 0.4
zonal_slope = 0.3
north_slope = 0.2

LANES = 128
GROUP = 8
F32 = jnp.float32
BF16 = jnp.bfloat16
MIB = 1024 * 1024
BAND = 32


def whole():
    return pl.BlockSpec(memory_space=pltpu.VMEM)


def anywhere():
    return pl.BlockSpec(memory_space=pl.ANY)


def full(*shape):
    return pl.BlockSpec(shape, lambda i: (0,) * len(shape))


def smem():
    return pl.BlockSpec(memory_space=pltpu.SMEM)


def struct(*shape):
    return jax.ShapeDtypeStruct(shape, F32)


def params(mib):
    return pltpu.CompilerParams(vmem_limit_bytes=mib * MIB)


def cost(microseconds):
    return pl.CostEstimate(
        flops=int(microseconds * 1e6), bytes_accessed=int(microseconds * 3.0e6), transcendentals=0
    )


def has_before(axis):
    return lax.axis_index(axis) > 0


def has_after(axis):
    return lax.axis_index(axis) < lax.axis_size(axis) - 1


def lane_ids(shape):
    return lax.broadcasted_iota(jnp.int32, shape, 1)


def row_ids(shape):
    return lax.broadcasted_iota(jnp.int32, shape, 0)


def edge_kernel(levels_ref, col_ref, row_ref):
    rows, cols = levels_ref.shape
    field = levels_ref[...].astype(F32)
    col_ref[...] = jnp.transpose(field)[cols - GROUP :]
    row_ref[...] = field[rows - GROUP :]


def edges(levels):
    rows, cols = levels.shape
    return pl.pallas_call(
        edge_kernel,
        grid=(1,),
        out_shape=(struct(GROUP, rows), struct(GROUP, cols)),
        in_specs=[full(rows, cols)],
        out_specs=(full(GROUP, rows), full(GROUP, cols)),
        compiler_params=params(4),
        cost_estimate=cost(1.0),
        name="edges",
    )(levels)


def rim_kernel(
    step,
    mix_ref,
    u_ref,
    v_ref,
    t_ref,
    east_ref,
    west_ref,
    north_ref,
    south_ref,
    top_ref,
    u_here,
    v_here,
    t_here,
    arrived,
):
    depth, rows, cols = u_ref.shape
    fields = ((u_ref, u_here), (v_ref, v_here), (t_ref, t_here))
    chunk = 2 * GROUP
    lane = lane_ids((chunk, cols))
    edge = (lane == 0) | (lane == cols - 1)

    def copy(f, at):
        levels = pl.ds(at * step, step)
        source, target = fields[f]
        return pltpu.make_async_copy(source.at[levels], target.at[levels], arrived.at[f, at])

    for at in range(depth // step):
        for f in range(3):
            copy(f, at).start()
    east_ref[...] = jnp.zeros((rows, cols), F32)
    west_ref[...] = jnp.zeros((rows, cols), F32)
    mix = mix_ref[...]
    rest = north_ref.shape[0] - 3 * BAND
    north_ref[3 * BAND :, :] = jnp.broadcast_to(mix[rows - 1 :], (rest, cols))
    south_ref[3 * BAND :, :] = jnp.broadcast_to(mix[:1], (rest, cols))

    def levels(at, carry):
        first = at * step
        flip = lax.rem(first, 2) == 1
        for f in range(3):
            copy(f, at).wait()

        def body(i, inner):
            here = pl.ds(pl.multiple_of(i * chunk, chunk), chunk)
            sums = [None, None]
            for k in range(step):
                for f in range(3):
                    value = jnp.where(edge, fields[f][1][first + k, here, :], 0.0)
                    moved = pltpu.roll(value, BAND * f + first + k + 1, 1)
                    sums[k % 2] = moved if sums[k % 2] is None else sums[k % 2] + moved
            east_ref[here, :] += jnp.where(flip, sums[1], sums[0])
            west_ref[here, :] += jnp.where(flip, sums[0], sums[1])
            return inner

        lax.fori_loop(0, rows // chunk, body, 0, unroll=8)
        return carry

    lax.fori_loop(0, depth // step, levels, 0)
    ids = lane_ids((rows, cols))
    even = lax.rem(ids, 2) == 0
    mix = pltpu.roll(mix, 3 * BAND + 1, 1)
    even_levels = east_ref[...]
    odd_levels = west_ref[...]
    east = jnp.where(even, even_levels, odd_levels)
    west = jnp.where(even, odd_levels, even_levels)
    east_ref[...] = jnp.where(ids == 3 * BAND, mix, east)
    west_ref[...] = jnp.where(ids == 3 * BAND + 1, mix, west)
    empty = jnp.zeros((BAND - depth, cols), F32)
    for f in range(3):
        band = slice(f * BAND, (f + 1) * BAND)
        here = fields[f][1]
        for out, place in ((north_ref, rows - 1), (south_ref, 0)):
            line = here[:, place : place + 1, :].reshape(depth, cols)
            out[band, :] = jnp.concatenate([line, empty], axis=0)
        top_ref[f] = here[0]


def rims(mixing, cots):
    depth, rows, cols = cots[0].shape
    step = 5
    lines = 3 * BAND + GROUP
    return pl.pallas_call(
        functools.partial(rim_kernel, step),
        out_shape=(struct(rows, cols),) * 2
        + (struct(lines, cols),) * 2
        + (struct(3, rows, cols),),
        in_specs=[whole()] + [anywhere()] * 3,
        out_specs=(whole(),) * 5,
        scratch_shapes=[pltpu.VMEM((depth, rows, cols), F32)] * 3
        + [pltpu.SemaphoreType.DMA((3, depth // step))],
        compiler_params=params(14),
        cost_estimate=cost(6.0),
        name="rims",
    )(mixing, *cots)


def surface_kernel(
    levels_ref,
    col_ref,
    row_ref,
    east_ref,
    west_ref,
    north_ref,
    south_ref,
    top_ref,
    out_ref,
    wet_c_ref,
    wet_u_ref,
    wet_v_ref,
    east_out_ref,
    west_out_ref,
    north_out_ref,
    south_out_ref,
):
    rows, cols = levels_ref.shape
    field = levels_ref[...].astype(F32)
    lane = lane_ids(field.shape)
    row = row_ids(field.shape)
    col = jnp.broadcast_to(jnp.transpose(col_ref[...])[:, GROUP - 1 :], field.shape)
    col = jnp.where(has_before("gx"), col, 0.0)
    west = jnp.where(lane == 0, col, pltpu.roll(field, 1, 1))
    line = jnp.broadcast_to(row_ref[GROUP - 1 :, :], field.shape)
    line = jnp.where(has_before("gy"), line, 0.0)
    south = jnp.where(row == 0, line, pltpu.roll(field, 1, 0))
    wet_u = jnp.minimum(field, west)
    wet_v = jnp.minimum(field, south)
    wets = (wet_u, wet_v, field)
    wet_c_ref[...] = field
    wet_u_ref[...] = wet_u
    wet_v_ref[...] = wet_v
    for comp in range(3):
        out_ref[comp] = jnp.where(wets[comp] > 0.0, time_step * top_ref[comp], 0.0)
    for ref, out, place, shift in (
        (east_ref, east_out_ref, cols - 1, 0),
        (west_ref, west_out_ref, 0, 1),
    ):
        at = lax.rem(lane + cols - shift, cols)
        band = at // BAND
        level = lax.rem(at, BAND).astype(F32)
        limit = [jnp.broadcast_to(wet[:, place : place + 1], field.shape) for wet in wets]
        limit = jnp.where(band == 0, limit[0], jnp.where(band == 1, limit[1], limit[2]))
        out[...] = jnp.where((level < limit) | (band == 3), ref[...], 0.0)
    level = row_ids((BAND, cols)).astype(F32)
    for ref, out, place in ((north_ref, north_out_ref, rows - 1), (south_ref, south_out_ref, 0)):
        out[3 * BAND :, :] = ref[3 * BAND :, :]
        for f in range(3):
            band = slice(f * BAND, (f + 1) * BAND)
            out[band, :] = jnp.where(level < wets[f][place : place + 1], ref[band, :], 0.0)


def surface(levels, col, row, packed):
    rows, cols = levels.shape
    rim = tuple(struct(*value.shape) for value in packed[:4])
    return pl.pallas_call(
        surface_kernel,
        out_shape=(struct(3, rows, cols),) + (struct(rows, cols),) * 3 + rim,
        in_specs=[whole()] * 8,
        out_specs=(whole(),) * 8,
        compiler_params=params(4),
        cost_estimate=cost(1.5),
        name="surface",
    )(levels, col, row, *packed)


def corner_kernel(north_ref, south_ref, east_ref, west_ref, north_out_ref, south_out_ref):
    spot = row_ids(north_ref.shape) == 3 * BAND + 1
    last = east_ref.shape[0] - 1
    corner = jnp.broadcast_to(east_ref[last:, :], north_ref.shape)
    north_out_ref[...] = jnp.where(spot, corner, north_ref[...])
    corner = jnp.broadcast_to(west_ref[:1, :], south_ref.shape)
    south_out_ref[...] = jnp.where(spot, corner, south_ref[...])


def corners(north, south, halo_e, halo_w):
    return pl.pallas_call(
        corner_kernel,
        out_shape=(struct(*north.shape),) * 2,
        in_specs=[whole()] * 4,
        out_specs=(whole(),) * 2,
        compiler_params=params(4),
        cost_estimate=cost(0.3),
        name="corners",
    )(north, south, halo_e, halo_w)


def adjoint_kernel(
    step,
    done,
    depth,
    total_rows,
    wet_c_ref,
    wet_u_ref,
    wet_v_ref,
    mix_ref,
    hw_ref,
    he_ref,
    hn_ref,
    hs_ref,
    old_refs,
    u_ref,
    v_ref,
    t_ref,
    gu_ref,
    gv_ref,
    gt_ref,
    state_ref,
    mix_n_ref,
    mix_s_ref,
    keep_ref,
    cor_ref,
    a_ref,
    b_ref,
    c_ref,
):
    rows, cols = mix_ref.shape
    at = pl.program_id(0)
    half = depth // 2
    first = depth - (done + at + 1) * step
    pad = GROUP
    cor_step = 0.25 * time_step * coriolis_base / total_rows
    slope_u = 0.5 * time_step * zonal_slope
    slope_v = 0.5 * time_step * north_slope
    weight = time_step * gravity_scale
    before_y, after_y = (has_before("gy"), has_after("gy"))

    @pl.when(at == 0)
    def _():
        shape = (rows, cols)
        lane = lane_ids(shape)
        row = row_ids(shape)
        start = lax.axis_index("gy") * rows
        lines = (row + start).astype(F32)
        cor = (0.25 * time_step * coriolis_base) * (0.5 + (lines + 0.5) / total_rows)
        cor_n = (0.25 * time_step * coriolis_base) * (0.5 + (lines + 1.5) / total_rows)
        cor_s = (0.25 * time_step * coriolis_base) * (0.5 + (lines - 0.5) / total_rows)
        cor_ref[...] = cor
        mix = mix_ref[...]
        keep_ref[...] = 1.0 - 4.0 * mix
        mix_n_ref[...] = jnp.where(
            row == rows - 1,
            jnp.broadcast_to(jnp.where(after_y, hn_ref[3 * BAND : 3 * BAND + 1, :], 0.0), shape),
            pltpu.roll(mix, rows - 1, 0),
        )
        mix_s_ref[...] = jnp.where(
            row == 0,
            jnp.broadcast_to(jnp.where(before_y, hs_ref[3 * BAND : 3 * BAND + 1, :], 0.0), shape),
            pltpu.roll(mix, 1, 0),
        )
        if old_refs:
            state_ref[...] = old_refs[0][...]
            return
        east = jnp.where(has_after("gx"), he_ref[...], 0.0)
        corner = hs_ref[3 * BAND + 1 : 3 * BAND + 2, :]
        corner = jnp.where(has_after("gx") & before_y, corner, 0.0)
        kind = lax.rem(lane + cols - 1, cols) // BAND
        mixed = east * jnp.broadcast_to(east[:, 3 * BAND + 1 : 3 * BAND + 2], shape)
        below = jnp.where(
            row == 0,
            jnp.broadcast_to(corner, shape),
            pltpu.roll(east, 1, 0),
        )
        turned = cor * east + cor_s * below
        total = jnp.where(kind == 0, east, 0.0)
        reach = 1
        while reach < depth:
            total = total + pltpu.roll(total, cols - reach, 1)
            reach *= 2
        from_e = (
            mixed
            + jnp.where(kind == 1, pltpu.roll(turned, BAND, 1), 0.0)
            + jnp.where(kind == 2, pltpu.roll(weight * total, 2 * BAND, 1), 0.0)
        )
        west = jnp.where(has_before("gx"), hw_ref[...], 0.0)
        corner = hn_ref[3 * BAND + 1 : 3 * BAND + 2, :]
        corner = jnp.where(has_before("gx") & after_y, corner, 0.0)
        kind = lane // BAND
        mixed = west * jnp.broadcast_to(west[:, 3 * BAND : 3 * BAND + 1], shape)
        above = jnp.where(
            row == rows - 1,
            jnp.broadcast_to(corner, shape),
            pltpu.roll(west, rows - 1, 0),
        )
        turned = cor * west + cor_n * above
        from_w = mixed - jnp.where(
            kind == 0,
            pltpu.roll(turned, cols - BAND, 1) + pltpu.roll(slope_u * west, cols - 2 * BAND, 1),
            0.0,
        )
        both = jnp.concatenate([from_e, from_w], axis=1)
        source = row_ids((2 * cols, 2 * cols))
        place = lane_ids((2 * cols, 2 * cols))
        part = place // cols
        spot = lax.rem(place, cols)
        pair = spot // 2
        slot = BAND * (pair // half) + part * half + lax.rem(pair, half)
        wanted = jnp.where(lax.rem(spot, 2) == 0, slot + 1, slot + cols)
        moves = jnp.where((source == wanted) & (pair < 3 * half), 1.0, 0.0).astype(BF16)
        moved = jnp.zeros((rows, 2 * cols), F32)
        for _ in range(3):
            high = both.astype(BF16)
            both = both - high.astype(F32)
            moved = moved + jnp.dot(high, moves, preferred_element_type=F32)
        state_ref[0] = moved[:, :cols]
        state_ref[1] = moved[:, cols:]
        state_ref[2] = jnp.zeros(shape, F32)
        state_ref[3] = jnp.zeros(shape, F32)

    fields = (
        (u_ref, wet_u_ref, a_ref),
        (v_ref, wet_v_ref, b_ref),
        (t_ref, wet_c_ref, c_ref),
    )

    def mask(i, carry):
        base = pl.multiple_of(i * 2 * GROUP, 2 * GROUP)
        here = pl.ds(base, 2 * GROUP)
        there = pl.ds(pl.multiple_of(base + pad, GROUP), 2 * GROUP)
        wets = [wet[here, :] for _, wet, _ in fields]
        for k in range(step):
            level = (first + k).astype(F32)
            for f, (ref, _, out) in enumerate(fields):
                out[k, there, :] = jnp.where(level < wets[f], ref[k, here, :], 0.0)
        return carry

    lax.fori_loop(0, rows // (2 * GROUP), mask, 0, unroll=8)
    for k in range(step):
        for f, (_, _, out) in enumerate(fields):
            slot = BAND * f + first + k
            out[k, pad - 1 : pad, :] = jnp.where(before_y, hs_ref[pl.ds(slot, 1), :], 0.0)
            out[k, pad + rows : pad + rows + 1, :] = jnp.where(
                after_y, hn_ref[pl.ds(slot, 1), :], 0.0
            )

    chunk = 2 * GROUP
    lane = lane_ids((chunk, cols))
    is_east = lane == cols - 1
    is_west = lane == 0
    part = (first >= half).astype(jnp.int32)

    def body(i, carry):
        base = pl.multiple_of(i * chunk, chunk)
        here = pl.ds(base, chunk)
        center = pl.ds(base + pad, chunk)
        north = pl.ds(base + pad + 1, chunk)
        south = pl.ds(base + pad - 1, chunk)
        mix = mix_ref[here, :]
        mix_n = mix_n_ref[here, :]
        mix_s = mix_s_ref[here, :]
        keep = keep_ref[here, :]
        cor = cor_ref[here, :]
        cor_n = cor + cor_step
        cor_s = cor - cor_step
        edges = state_ref[part, here, :]
        sum_a = state_ref[2, here, :]
        sum_d = state_ref[3, here, :]
        for k in reversed(range(step)):
            inner = first + k - part * half

            def both_sides(west, east, f, inner=inner):
                edge = pltpu.roll(edges, 2 * cols - 1 - 2 * (f * half + inner), 1)
                return jnp.where(is_west, edge, pltpu.roll(west, 1, 1)) + jnp.where(
                    is_east, edge, pltpu.roll(east, cols - 1, 1)
                )

            a = a_ref[k, center, :]
            a_n = a_ref[k, north, :]
            a_s = a_ref[k, south, :]
            b = b_ref[k, center, :]
            b_n = b_ref[k, north, :]
            b_s = b_ref[k, south, :]
            c = c_ref[k, center, :]
            c_n = c_ref[k, north, :]
            c_s = c_ref[k, south, :]
            mix_a = mix * a
            turn_b = cor * b + cor_n * b_n + slope_u * c
            gu_ref[k, here, :] = (
                keep * a
                + (mix_n * a_n + mix_s * a_s)
                - turn_b
                + both_sides(mix_a - turn_b, mix_a, 0)
            )
            mix_b = mix * b
            turn_a = cor * a + cor_s * a_s
            gv_ref[k, here, :] = (
                keep * b
                + (mix_n * b_n + mix_s * b_s)
                + (turn_a - slope_v * (c + c_s))
                + both_sides(mix_b, mix_b + turn_a, 1)
            )
            mix_c = mix * c
            sum_a = sum_a + weight * a
            sum_d = sum_d + weight * (b - b_n)
            gt_ref[k, here, :] = (
                keep * c
                + (mix_n * c_n + mix_s * c_s)
                - (sum_a + sum_d)
                + both_sides(mix_c, mix_c + sum_a, 2)
            )
        state_ref[2, here, :] = sum_a
        state_ref[3, here, :] = sum_d
        return carry

    lax.fori_loop(0, rows // chunk, body, 0, unroll=rows // chunk)


def adjoint(planes, halos, cots, after, total_rows, earlier=None):
    depth, rows, cols = cots[0].shape
    step = 5
    first = depth // (3 * step)
    done, steps = (0, first) if earlier is None else (first, depth // step - first)
    plane = full(rows, cols)
    top = depth // step - 1 - done
    block = pl.BlockSpec((step, rows, cols), lambda i: (top - i, 0, 0))
    grads, state = ((), ()) if earlier is None else earlier
    n_planes = len(planes) + len(halos)
    n_state = len(state)
    kept = (4, rows, cols)

    def kernel(*refs):
        front, refs = refs[:n_planes], refs[n_planes:]
        old, refs = refs[:n_state], refs[n_state:]
        ins, refs = refs[:3], refs[3 + 1 + len(grads) :]
        adjoint_kernel(step, done, depth, total_rows, *front, old, *ins, *refs)

    padded = pltpu.VMEM((step, rows + 2 * GROUP, cols), F32)
    aliases = {n_planes + n_state + 4 + i: i for i in range(len(grads))}
    result = pl.pallas_call(
        kernel,
        grid=(steps,),
        out_shape=(struct(depth, rows, cols),) * 3 + (struct(*kept),),
        in_specs=[plane] * len(planes)
        + [full(*halo.shape) for halo in halos]
        + [full(*kept)] * n_state
        + [block] * 3
        + [anywhere()] * (1 + len(grads)),
        out_specs=(block,) * 3 + (full(*kept),),
        scratch_shapes=[pltpu.VMEM((rows, cols), F32)] * 4 + [padded] * 3,
        input_output_aliases=aliases,
        compiler_params=params(16),
        cost_estimate=cost(3.0 * steps),
        name="adjoint",
    )(*planes, *halos, *state, *cots, after, *grads)
    return result[:3], result[3:]


def halves(value):
    high = value.astype(BF16)
    return high, (value - high.astype(F32)).astype(BF16)


def product(blocks, fields, field_first):
    axis = 1 if field_first else 0
    block_high, block_low = (jnp.concatenate([b[i] for b in blocks], axis=1) for i in range(2))
    field_high, field_low = (jnp.concatenate([f[i] for f in fields], axis=axis) for i in range(2))
    if field_first:
        first, second = (field_high, field_low), (block_high, block_low)
    else:
        first, second = (block_high, block_low), (field_high, field_low)
    dims = (((1,), (axis,)), ((), ()))
    both = lax.dot_general(
        jnp.concatenate(first, axis=0), second[0], dims, preferred_element_type=F32
    )
    last = lax.dot_general(first[0], second[1], dims, preferred_element_type=F32)
    size = first[0].shape[0]
    return both[:size] + (both[size:] + last)


def zonal_kernel(pattern_ref, blocks_ref, field_ref, after_ref, out_ref, high_ref, low_ref):
    for tile in range(field_ref.shape[0]):
        high_ref[tile], low_ref[tile] = halves(field_ref[tile])
    for r in range(blocks_ref.shape[0]):
        entries = range(blocks_ref.shape[1])
        picked = [pattern_ref[r, j] for j in entries]
        out_ref[r] = product(
            [halves(blocks_ref[r, j]) for j in entries],
            [(high_ref[p], low_ref[p]) for p in picked],
            True,
        )


def zonal(pattern, blocks, field, after):
    return pl.pallas_call(
        zonal_kernel,
        out_shape=struct(*field.shape),
        in_specs=[smem()] + [whole()] * 2 + [anywhere()],
        out_specs=whole(),
        scratch_shapes=[pltpu.VMEM(field.shape, BF16)] * 2,
        compiler_params=params(6),
        cost_estimate=cost(2.0),
        name="zonal",
    )(pattern, blocks, field, after)


def meridional_kernel(pattern_ref, blocks_ref, field_refs, out_ref, high_ref, low_ref):
    _, block, _ = high_ref.shape
    _, rows, cols = field_refs[0].shape
    chunk = out_ref.shape[1] // 3
    mine = rows // block
    me = lax.axis_index("gy")
    for m, ref in enumerate(field_refs):
        first = (me ^ m) * mine
        for h in range(mine):
            here = slice(h * block, (h + 1) * block)
            value = jnp.concatenate([ref[c, here, :] for c in range(3)], axis=1)
            high_ref[first + h], low_ref[first + h] = halves(value)
    entries = range(blocks_ref.shape[1])
    for h in range(mine):
        r = me * mine + h
        picked = [pattern_ref[r, j] for j in entries]
        result = product(
            [halves(blocks_ref[r, j]) for j in entries],
            [(high_ref[p], low_ref[p]) for p in picked],
            False,
        )
        for line in range(0, block, chunk):
            part = (h * block + line) // chunk
            for c in range(3):
                out_ref[part, c * chunk : (c + 1) * chunk, :] = result[
                    line : line + chunk, c * cols : (c + 1) * cols
                ]


def meridional(pattern, blocks, fields, parts):
    n = len(fields)
    _, rows, cols = fields[0].shape
    tiles, _, block, _ = blocks.shape

    def kernel(pattern_ref, blocks_ref, *refs):
        meridional_kernel(pattern_ref, blocks_ref, refs[:n], *refs[n:])

    return pl.pallas_call(
        kernel,
        out_shape=struct(parts, 3 * rows // parts, cols),
        in_specs=[smem()] + [whole()] * (1 + n),
        out_specs=whole(),
        scratch_shapes=[pltpu.VMEM((tiles, block, 3 * cols), BF16)] * 2,
        compiler_params=params(4 + n),
        cost_estimate=cost(2.0),
        name="meridional",
    )(pattern, blocks, *fields)


def finish_kernel(field_ref, after_ref, out_ref):
    parts, height, cols = field_ref.shape
    chunk = height // 3
    for part in range(parts):
        for c in range(3):
            out_ref[c, part * chunk : (part + 1) * chunk, :] = field_ref[
                part, c * chunk : (c + 1) * chunk, :
            ]


def finish(field, after):
    parts, height, cols = field.shape
    return pl.pallas_call(
        finish_kernel,
        out_shape=struct(3, parts * height // 3, cols),
        in_specs=[whole(), anywhere()],
        out_specs=whole(),
        compiler_params=params(4),
        cost_estimate=cost(0.7),
        name="finish",
    )(field, after)


def shards(cot_u, cot_v, cot_t, levels, mixing, pattern_x, blocks_x, pattern_y, blocks_y):
    depth, rows, cols = cot_u.shape
    nx, ny = (lax.axis_size("gx"), lax.axis_size("gy"))
    up_x = [(i, (i + 1) % nx) for i in range(nx)]
    down_x = [(j, i) for i, j in up_x]
    up_y = [(i, (i + 1) % ny) for i in range(ny)]
    down_y = [(j, i) for i, j in up_y]

    mixing = pltpu.with_memory_space_constraint(mixing, pltpu.HBM)
    cots = tuple(pltpu.with_memory_space_constraint(c, pltpu.HBM) for c in (cot_u, cot_v, cot_t))
    level_col, level_row = edges(levels)
    level_col = lax.ppermute(level_col, "gx", up_x)
    level_row = lax.ppermute(level_row, "gy", up_y)
    packed = rims(mixing, cots)
    field, wet_c, wet_u, wet_v, east, west, north, south = surface(
        levels, level_col, level_row, packed
    )
    halo_w = lax.ppermute(east, "gx", up_x)
    halo_e = lax.ppermute(west, "gx", down_x)
    tiles = {0: field}
    bit = ny // 2
    bit = 1
    while bit < ny:
        tiles[bit] = lax.ppermute(field, "gy", [(i, i ^ bit) for i in range(ny)])
        bit *= 2
    own = [m for m in tiles if m]
    *received, halo_w, halo_e = lax.optimization_barrier(
        (*(tiles[m] for m in own), halo_w, halo_e)
    )
    tiles.update(zip(own, received))
    bit = ny // 4
    while bit:
        for m in sorted(m for m in tiles if m and m % (2 * bit) == 0):
            tiles[m ^ bit] = lax.ppermute(tiles[m], "gy", [(i, i ^ bit) for i in range(ny)])
        bit //= 2
    north, south = corners(north, south, halo_e, halo_w)
    halo_s = lax.ppermute(north, "gy", up_y)
    halo_n = lax.ppermute(south, "gy", down_y)
    mixed = meridional(pattern_y, blocks_y, [tiles[m] for m in range(ny)], nx)
    mixed, halo_s, halo_n = lax.optimization_barrier((mixed, halo_s, halo_n))
    lines = lax.all_to_all(mixed, "gx", 0, 0)
    planes = (wet_c, wet_u, wet_v, mixing)
    halos = (halo_w, halo_e, halo_n, halo_s)
    grads, state = adjoint(planes, halos, cots, mixed, rows * ny)
    turned = zonal(pattern_x, blocks_x, lines, state[0])
    back = lax.all_to_all(turned, "gx", 0, 0)
    grads = tuple(pltpu.with_memory_space_constraint(g, pltpu.HBM) for g in grads)
    grads, token = adjoint(planes, halos, cots, turned, rows * ny, (grads, state))
    return (*grads, finish(back, token[0]))


def solution(mesh):
    grid = P(None, "gy", "gx")
    flat = P("gy", "gx")
    return jax.shard_map(
        shards,
        mesh=mesh,
        in_specs=(grid, grid, grid, flat, flat, P(), P(), P(), P()),
        out_specs=(grid, grid, grid, grid),
        check_vma=False,
    )
```

```python
import functools

import jax
import jax.numpy as jnp
from jax import lax
from jax.experimental import pallas as pl
from jax.experimental.pallas import tpu as pltpu
from jax.sharding import PartitionSpec as P

time_step = 0.5
gravity_scale = 0.05
coriolis_base = 0.4
zonal_slope = 0.3
north_slope = 0.2

LANES = 128
GROUP = 8
F32 = jnp.float32
BF16 = jnp.bfloat16
MIB = 1024 * 1024
BAND = 32


def whole():
    return pl.BlockSpec(memory_space=pltpu.VMEM)


def anywhere():
    return pl.BlockSpec(memory_space=pl.ANY)


def full(*shape):
    return pl.BlockSpec(shape, lambda i: (0,) * len(shape))


def smem():
    return pl.BlockSpec(memory_space=pltpu.SMEM)


def struct(*shape):
    return jax.ShapeDtypeStruct(shape, F32)


def params(mib):
    return pltpu.CompilerParams(vmem_limit_bytes=mib * MIB)


def cost(microseconds):
    return pl.CostEstimate(
        flops=int(microseconds * 1e6), bytes_accessed=int(microseconds * 3.0e6), transcendentals=0
    )


def has_before(axis):
    return lax.axis_index(axis) > 0


def has_after(axis):
    return lax.axis_index(axis) < lax.axis_size(axis) - 1


def opposite(part, parts):
    return (part + parts // 2) % parts


def lane_ids(shape):
    return lax.broadcasted_iota(jnp.int32, shape, 1)


def row_ids(shape):
    return lax.broadcasted_iota(jnp.int32, shape, 0)


def edge_kernel(levels_ref, col_ref, row_ref):
    rows, cols = levels_ref.shape
    field = levels_ref[...].astype(F32)
    col_ref[...] = jnp.transpose(field)[cols - GROUP :]
    row_ref[...] = field[rows - GROUP :]


def edges(levels):
    rows, cols = levels.shape
    return pl.pallas_call(
        edge_kernel,
        grid=(1,),
        out_shape=(struct(GROUP, rows), struct(GROUP, cols)),
        in_specs=[full(rows, cols)],
        out_specs=(full(GROUP, rows), full(GROUP, cols)),
        compiler_params=params(4),
        cost_estimate=cost(1.0),
        name="edges",
    )(levels)


def rim_kernel(
    step,
    mix_ref,
    u_ref,
    v_ref,
    t_ref,
    east_ref,
    west_ref,
    north_ref,
    south_ref,
    top_ref,
    u_here,
    v_here,
    t_here,
    arrived,
):
    depth, rows, cols = u_ref.shape
    fields = ((u_ref, u_here), (v_ref, v_here), (t_ref, t_here))
    chunk = 2 * GROUP
    lane = lane_ids((chunk, cols))
    edge = (lane == 0) | (lane == cols - 1)

    def copy(f, at):
        levels = pl.ds(at * step, step)
        source, target = fields[f]
        return pltpu.make_async_copy(source.at[levels], target.at[levels], arrived.at[f, at])

    for at in range(depth // step):
        for f in range(3):
            copy(f, at).start()
    east_ref[...] = jnp.zeros((rows, cols), F32)
    west_ref[...] = jnp.zeros((rows, cols), F32)
    mix = mix_ref[...]
    rest = north_ref.shape[0] - 3 * BAND
    north_ref[3 * BAND :, :] = jnp.broadcast_to(mix[rows - 1 :], (rest, cols))
    south_ref[3 * BAND :, :] = jnp.broadcast_to(mix[:1], (rest, cols))

    def levels(at, carry):
        first = at * step
        flip = lax.rem(first, 2) == 1
        for f in range(3):
            copy(f, at).wait()

        def body(i, inner):
            here = pl.ds(pl.multiple_of(i * chunk, chunk), chunk)
            sums = [None, None]
            for k in range(step):
                for f in range(3):
                    value = jnp.where(edge, fields[f][1][first + k, here, :], 0.0)
                    moved = pltpu.roll(value, BAND * f + first + k + 1, 1)
                    sums[k % 2] = moved if sums[k % 2] is None else sums[k % 2] + moved
            east_ref[here, :] += jnp.where(flip, sums[1], sums[0])
            west_ref[here, :] += jnp.where(flip, sums[0], sums[1])
            return inner

        lax.fori_loop(0, rows // chunk, body, 0, unroll=8)
        return carry

    lax.fori_loop(0, depth // step, levels, 0)
    ids = lane_ids((rows, cols))
    even = lax.rem(ids, 2) == 0
    mix = pltpu.roll(mix, 3 * BAND + 1, 1)
    even_levels = east_ref[...]
    odd_levels = west_ref[...]
    east = jnp.where(even, even_levels, odd_levels)
    west = jnp.where(even, odd_levels, even_levels)
    east_ref[...] = jnp.where(ids == 3 * BAND, mix, east)
    west_ref[...] = jnp.where(ids == 3 * BAND + 1, mix, west)
    empty = jnp.zeros((BAND - depth, cols), F32)
    for f in range(3):
        band = slice(f * BAND, (f + 1) * BAND)
        here = fields[f][1]
        for out, place in ((north_ref, rows - 1), (south_ref, 0)):
            line = here[:, place : place + 1, :].reshape(depth, cols)
            out[band, :] = jnp.concatenate([line, empty], axis=0)
        top_ref[f] = here[0]


def rims(mixing, cots):
    depth, rows, cols = cots[0].shape
    step = 5
    lines = 3 * BAND + GROUP
    return pl.pallas_call(
        functools.partial(rim_kernel, step),
        out_shape=(struct(rows, cols),) * 2
        + (struct(lines, cols),) * 2
        + (struct(3, rows, cols),),
        in_specs=[whole()] + [anywhere()] * 3,
        out_specs=(whole(),) * 5,
        scratch_shapes=[pltpu.VMEM((depth, rows, cols), F32)] * 3
        + [pltpu.SemaphoreType.DMA((3, depth // step))],
        compiler_params=params(14),
        cost_estimate=cost(6.0),
        name="rims",
    )(mixing, *cots)


def surface_kernel(
    levels_ref,
    col_ref,
    row_ref,
    east_ref,
    west_ref,
    north_ref,
    south_ref,
    top_ref,
    out_ref,
    wet_c_ref,
    wet_u_ref,
    wet_v_ref,
    east_out_ref,
    west_out_ref,
    north_out_ref,
    south_out_ref,
):
    rows, cols = levels_ref.shape
    field = levels_ref[...].astype(F32)
    lane = lane_ids(field.shape)
    row = row_ids(field.shape)
    col = jnp.broadcast_to(jnp.transpose(col_ref[...])[:, GROUP - 1 :], field.shape)
    col = jnp.where(has_before("gx"), col, 0.0)
    west = jnp.where(lane == 0, col, pltpu.roll(field, 1, 1))
    line = jnp.broadcast_to(row_ref[GROUP - 1 :, :], field.shape)
    line = jnp.where(has_before("gy"), line, 0.0)
    south = jnp.where(row == 0, line, pltpu.roll(field, 1, 0))
    wet_u = jnp.minimum(field, west)
    wet_v = jnp.minimum(field, south)
    wets = (wet_u, wet_v, field)
    wet_c_ref[...] = field
    wet_u_ref[...] = wet_u
    wet_v_ref[...] = wet_v
    for comp in range(3):
        out_ref[comp] = jnp.where(wets[comp] > 0.0, time_step * top_ref[comp], 0.0)
    for ref, out, place, shift in (
        (east_ref, east_out_ref, cols - 1, 0),
        (west_ref, west_out_ref, 0, 1),
    ):
        at = lax.rem(lane + cols - shift, cols)
        band = at // BAND
        level = lax.rem(at, BAND).astype(F32)
        limit = [jnp.broadcast_to(wet[:, place : place + 1], field.shape) for wet in wets]
        limit = jnp.where(band == 0, limit[0], jnp.where(band == 1, limit[1], limit[2]))
        out[...] = jnp.where((level < limit) | (band == 3), ref[...], 0.0)
    level = row_ids((BAND, cols)).astype(F32)
    for ref, out, place in ((north_ref, north_out_ref, rows - 1), (south_ref, south_out_ref, 0)):
        out[3 * BAND :, :] = ref[3 * BAND :, :]
        for f in range(3):
            band = slice(f * BAND, (f + 1) * BAND)
            out[band, :] = jnp.where(level < wets[f][place : place + 1], ref[band, :], 0.0)


def surface(levels, col, row, packed):
    rows, cols = levels.shape
    rim = tuple(struct(*value.shape) for value in packed[:4])
    return pl.pallas_call(
        surface_kernel,
        out_shape=(struct(3, rows, cols),) + (struct(rows, cols),) * 3 + rim,
        in_specs=[whole()] * 8,
        out_specs=(whole(),) * 8,
        compiler_params=params(4),
        cost_estimate=cost(1.5),
        name="surface",
    )(levels, col, row, *packed)


def corner_kernel(north_ref, south_ref, east_ref, west_ref, north_out_ref, south_out_ref):
    spot = row_ids(north_ref.shape) == 3 * BAND + 1
    last = east_ref.shape[0] - 1
    corner = jnp.broadcast_to(east_ref[last:, :], north_ref.shape)
    north_out_ref[...] = jnp.where(spot, corner, north_ref[...])
    corner = jnp.broadcast_to(west_ref[:1, :], south_ref.shape)
    south_out_ref[...] = jnp.where(spot, corner, south_ref[...])


def corners(north, south, halo_e, halo_w):
    return pl.pallas_call(
        corner_kernel,
        out_shape=(struct(*north.shape),) * 2,
        in_specs=[whole()] * 4,
        out_specs=(whole(),) * 2,
        compiler_params=params(4),
        cost_estimate=cost(0.3),
        name="corners",
    )(north, south, halo_e, halo_w)


def adjoint_kernel(
    step,
    done,
    depth,
    total_rows,
    wet_c_ref,
    wet_u_ref,
    wet_v_ref,
    mix_ref,
    hw_ref,
    he_ref,
    hn_ref,
    hs_ref,
    old_refs,
    u_ref,
    v_ref,
    t_ref,
    gu_ref,
    gv_ref,
    gt_ref,
    state_ref,
    mix_n_ref,
    mix_s_ref,
    keep_ref,
    cor_ref,
    a_ref,
    b_ref,
    c_ref,
):
    rows, cols = mix_ref.shape
    at = pl.program_id(0)
    half = depth // 2
    first = depth - (done + at + 1) * step
    pad = GROUP
    cor_step = 0.25 * time_step * coriolis_base / total_rows
    slope_u = 0.5 * time_step * zonal_slope
    slope_v = 0.5 * time_step * north_slope
    weight = time_step * gravity_scale
    before_y, after_y = (has_before("gy"), has_after("gy"))

    @pl.when(at == 0)
    def _():
        shape = (rows, cols)
        lane = lane_ids(shape)
        row = row_ids(shape)
        start = lax.axis_index("gy") * rows
        lines = (row + start).astype(F32)
        cor = (0.25 * time_step * coriolis_base) * (0.5 + (lines + 0.5) / total_rows)
        cor_n = (0.25 * time_step * coriolis_base) * (0.5 + (lines + 1.5) / total_rows)
        cor_s = (0.25 * time_step * coriolis_base) * (0.5 + (lines - 0.5) / total_rows)
        cor_ref[...] = cor
        mix = mix_ref[...]
        keep_ref[...] = 1.0 - 4.0 * mix
        mix_n_ref[...] = jnp.where(
            row == rows - 1,
            jnp.broadcast_to(jnp.where(after_y, hn_ref[3 * BAND : 3 * BAND + 1, :], 0.0), shape),
            pltpu.roll(mix, rows - 1, 0),
        )
        mix_s_ref[...] = jnp.where(
            row == 0,
            jnp.broadcast_to(jnp.where(before_y, hs_ref[3 * BAND : 3 * BAND + 1, :], 0.0), shape),
            pltpu.roll(mix, 1, 0),
        )
        if old_refs:
            state_ref[...] = old_refs[0][...]
            return
        east = jnp.where(has_after("gx"), he_ref[...], 0.0)
        corner = hs_ref[3 * BAND + 1 : 3 * BAND + 2, :]
        corner = jnp.where(has_after("gx") & before_y, corner, 0.0)
        kind = lax.rem(lane + cols - 1, cols) // BAND
        mixed = east * jnp.broadcast_to(east[:, 3 * BAND + 1 : 3 * BAND + 2], shape)
        below = jnp.where(
            row == 0,
            jnp.broadcast_to(corner, shape),
            pltpu.roll(east, 1, 0),
        )
        turned = cor * east + cor_s * below
        total = jnp.where(kind == 0, east, 0.0)
        reach = 1
        while reach < depth:
            total = total + pltpu.roll(total, cols - reach, 1)
            reach *= 2
        from_e = (
            mixed
            + jnp.where(kind == 1, pltpu.roll(turned, BAND, 1), 0.0)
            + jnp.where(kind == 2, pltpu.roll(weight * total, 2 * BAND, 1), 0.0)
        )
        west = jnp.where(has_before("gx"), hw_ref[...], 0.0)
        corner = hn_ref[3 * BAND + 1 : 3 * BAND + 2, :]
        corner = jnp.where(has_before("gx") & after_y, corner, 0.0)
        kind = lane // BAND
        mixed = west * jnp.broadcast_to(west[:, 3 * BAND : 3 * BAND + 1], shape)
        above = jnp.where(
            row == rows - 1,
            jnp.broadcast_to(corner, shape),
            pltpu.roll(west, rows - 1, 0),
        )
        turned = cor * west + cor_n * above
        from_w = mixed - jnp.where(
            kind == 0,
            pltpu.roll(turned, cols - BAND, 1) + pltpu.roll(slope_u * west, cols - 2 * BAND, 1),
            0.0,
        )
        both = jnp.concatenate([from_e, from_w], axis=1)
        source = row_ids((2 * cols, 2 * cols))
        place = lane_ids((2 * cols, 2 * cols))
        part = place // cols
        spot = lax.rem(place, cols)
        pair = spot // 2
        slot = BAND * (pair // half) + part * half + lax.rem(pair, half)
        wanted = jnp.where(lax.rem(spot, 2) == 0, slot + 1, slot + cols)
        moves = jnp.where((source == wanted) & (pair < 3 * half), 1.0, 0.0).astype(BF16)
        moved = jnp.zeros((rows, 2 * cols), F32)
        for _ in range(3):
            high = both.astype(BF16)
            both = both - high.astype(F32)
            moved = moved + jnp.dot(high, moves, preferred_element_type=F32)
        state_ref[0] = moved[:, :cols]
        state_ref[1] = moved[:, cols:]
        state_ref[2] = jnp.zeros(shape, F32)
        state_ref[3] = jnp.zeros(shape, F32)

    fields = (
        (u_ref, wet_u_ref, a_ref),
        (v_ref, wet_v_ref, b_ref),
        (t_ref, wet_c_ref, c_ref),
    )

    def mask(i, carry):
        base = pl.multiple_of(i * 2 * GROUP, 2 * GROUP)
        here = pl.ds(base, 2 * GROUP)
        there = pl.ds(pl.multiple_of(base + pad, GROUP), 2 * GROUP)
        wets = [wet[here, :] for _, wet, _ in fields]
        for k in range(step):
            level = (first + k).astype(F32)
            for f, (ref, _, out) in enumerate(fields):
                out[k, there, :] = jnp.where(level < wets[f], ref[k, here, :], 0.0)
        return carry

    lax.fori_loop(0, rows // (2 * GROUP), mask, 0, unroll=8)
    for k in range(step):
        for f, (_, _, out) in enumerate(fields):
            slot = BAND * f + first + k
            out[k, pad - 1 : pad, :] = jnp.where(before_y, hs_ref[pl.ds(slot, 1), :], 0.0)
            out[k, pad + rows : pad + rows + 1, :] = jnp.where(
                after_y, hn_ref[pl.ds(slot, 1), :], 0.0
            )

    chunk = 2 * GROUP
    lane = lane_ids((chunk, cols))
    is_east = lane == cols - 1
    is_west = lane == 0
    part = (first >= half).astype(jnp.int32)

    def body(i, carry):
        base = pl.multiple_of(i * chunk, chunk)
        here = pl.ds(base, chunk)
        center = pl.ds(base + pad, chunk)
        north = pl.ds(base + pad + 1, chunk)
        south = pl.ds(base + pad - 1, chunk)
        mix = mix_ref[here, :]
        mix_n = mix_n_ref[here, :]
        mix_s = mix_s_ref[here, :]
        keep = keep_ref[here, :]
        cor = cor_ref[here, :]
        cor_n = cor + cor_step
        cor_s = cor - cor_step
        edges = state_ref[part, here, :]
        sum_a = state_ref[2, here, :]
        sum_d = state_ref[3, here, :]
        for k in reversed(range(step)):
            inner = first + k - part * half

            def both_sides(west, east, f, inner=inner):
                edge = pltpu.roll(edges, 2 * cols - 1 - 2 * (f * half + inner), 1)
                return jnp.where(is_west, edge, pltpu.roll(west, 1, 1)) + jnp.where(
                    is_east, edge, pltpu.roll(east, cols - 1, 1)
                )

            a = a_ref[k, center, :]
            a_n = a_ref[k, north, :]
            a_s = a_ref[k, south, :]
            b = b_ref[k, center, :]
            b_n = b_ref[k, north, :]
            b_s = b_ref[k, south, :]
            c = c_ref[k, center, :]
            c_n = c_ref[k, north, :]
            c_s = c_ref[k, south, :]
            mix_a = mix * a
            turn_b = cor * b + cor_n * b_n + slope_u * c
            gu_ref[k, here, :] = (
                keep * a
                + (mix_n * a_n + mix_s * a_s)
                - turn_b
                + both_sides(mix_a - turn_b, mix_a, 0)
            )
            mix_b = mix * b
            turn_a = cor * a + cor_s * a_s
            gv_ref[k, here, :] = (
                keep * b
                + (mix_n * b_n + mix_s * b_s)
                + (turn_a - slope_v * (c + c_s))
                + both_sides(mix_b, mix_b + turn_a, 1)
            )
            mix_c = mix * c
            sum_a = sum_a + weight * a
            sum_d = sum_d + weight * (b - b_n)
            gt_ref[k, here, :] = (
                keep * c
                + (mix_n * c_n + mix_s * c_s)
                - (sum_a + sum_d)
                + both_sides(mix_c, mix_c + sum_a, 2)
            )
        state_ref[2, here, :] = sum_a
        state_ref[3, here, :] = sum_d
        return carry

    lax.fori_loop(0, rows // chunk, body, 0, unroll=rows // chunk)


def adjoint(planes, halos, cots, after, total_rows, earlier=None):
    depth, rows, cols = cots[0].shape
    step = 5
    first = depth // (2 * step)
    done, steps = (0, first) if earlier is None else (first, depth // step - first)
    plane = full(rows, cols)
    top = depth // step - 1 - done
    block = pl.BlockSpec((step, rows, cols), lambda i: (top - i, 0, 0))
    grads, state = ((), ()) if earlier is None else earlier
    n_planes = len(planes) + len(halos)
    n_state = len(state)
    kept = (4, rows, cols)

    def kernel(*refs):
        front, refs = refs[:n_planes], refs[n_planes:]
        old, refs = refs[:n_state], refs[n_state:]
        ins, refs = refs[:3], refs[3 + 1 + len(grads) :]
        adjoint_kernel(step, done, depth, total_rows, *front, old, *ins, *refs)

    padded = pltpu.VMEM((step, rows + 2 * GROUP, cols), F32)
    aliases = {n_planes + n_state + 4 + i: i for i in range(len(grads))}
    result = pl.pallas_call(
        kernel,
        grid=(steps,),
        out_shape=(struct(depth, rows, cols),) * 3 + (struct(*kept),),
        in_specs=[plane] * len(planes)
        + [full(*halo.shape) for halo in halos]
        + [full(*kept)] * n_state
        + [block] * 3
        + [anywhere()] * (1 + len(grads)),
        out_specs=(block,) * 3 + (full(*kept),),
        scratch_shapes=[pltpu.VMEM((rows, cols), F32)] * 4 + [padded] * 3,
        input_output_aliases=aliases,
        compiler_params=params(16),
        cost_estimate=cost(3.0 * steps),
        name="adjoint",
    )(*planes, *halos, *state, *cots, after, *grads)
    return result[:3], result[3:]


def halves(value):
    high = value.astype(BF16)
    return high, (value - high.astype(F32)).astype(BF16)


def product(blocks, fields, field_first):
    axis = 1 if field_first else 0
    block_high, block_low = (jnp.concatenate([b[i] for b in blocks], axis=1) for i in range(2))
    field_high, field_low = (jnp.concatenate([f[i] for f in fields], axis=axis) for i in range(2))
    if field_first:
        first, second = (field_high, field_low), (block_high, block_low)
    else:
        first, second = (block_high, block_low), (field_high, field_low)
    dims = (((1,), (axis,)), ((), ()))
    both = lax.dot_general(
        jnp.concatenate(first, axis=0), second[0], dims, preferred_element_type=F32
    )
    last = lax.dot_general(first[0], second[1], dims, preferred_element_type=F32)
    size = first[0].shape[0]
    return both[:size] + (both[size:] + last)


def zonal_kernel(pattern_ref, blocks_ref, field_ref, after_ref, out_ref, high_ref, low_ref):
    for slot in range(field_ref.shape[0]):
        tile = opposite(slot, field_ref.shape[0])
        high_ref[tile], low_ref[tile] = halves(field_ref[slot])
    for r in range(blocks_ref.shape[0]):
        entries = range(blocks_ref.shape[1])
        picked = [pattern_ref[r, j] for j in entries]
        out_ref[opposite(r, out_ref.shape[0])] = product(
            [halves(blocks_ref[r, j]) for j in entries],
            [(high_ref[p], low_ref[p]) for p in picked],
            True,
        )


def zonal(pattern, blocks, field, after):
    return pl.pallas_call(
        zonal_kernel,
        out_shape=struct(*field.shape),
        in_specs=[smem()] + [whole()] * 2 + [anywhere()],
        out_specs=whole(),
        scratch_shapes=[pltpu.VMEM(field.shape, BF16)] * 2,
        compiler_params=params(6),
        cost_estimate=cost(2.0),
        name="zonal",
    )(pattern, blocks, field, after)


def meridional_kernel(pattern_ref, blocks_ref, field_refs, out_ref, high_ref, low_ref):
    _, block, _ = high_ref.shape
    _, rows, cols = field_refs[0].shape
    chunk = out_ref.shape[1] // 3
    mine = rows // block
    me = lax.axis_index("gy")
    for m, ref in enumerate(field_refs):
        first = (me ^ m) * mine
        for h in range(mine):
            here = slice(h * block, (h + 1) * block)
            value = jnp.concatenate([ref[c, here, :] for c in range(3)], axis=1)
            high_ref[first + h], low_ref[first + h] = halves(value)
    entries = range(blocks_ref.shape[1])
    for h in range(mine):
        r = me * mine + h
        picked = [pattern_ref[r, j] for j in entries]
        result = product(
            [halves(blocks_ref[r, j]) for j in entries],
            [(high_ref[p], low_ref[p]) for p in picked],
            False,
        )
        for line in range(0, block, chunk):
            part = (h * block + line) // chunk
            for c in range(3):
                out_ref[opposite(part, out_ref.shape[0]), c * chunk : (c + 1) * chunk, :] = result[
                    line : line + chunk, c * cols : (c + 1) * cols
                ]


def meridional(pattern, blocks, fields, parts):
    n = len(fields)
    _, rows, cols = fields[0].shape
    tiles, _, block, _ = blocks.shape

    def kernel(pattern_ref, blocks_ref, *refs):
        meridional_kernel(pattern_ref, blocks_ref, refs[:n], *refs[n:])

    return pl.pallas_call(
        kernel,
        out_shape=struct(parts, 3 * rows // parts, cols),
        in_specs=[smem()] + [whole()] * (1 + n),
        out_specs=whole(),
        scratch_shapes=[pltpu.VMEM((tiles, block, 3 * cols), BF16)] * 2,
        compiler_params=params(4 + n),
        cost_estimate=cost(2.0),
        name="meridional",
    )(pattern, blocks, *fields)


def finish_kernel(field_ref, after_ref, out_ref):
    parts, height, cols = field_ref.shape
    chunk = height // 3
    for part in range(parts):
        for c in range(3):
            out_ref[c, part * chunk : (part + 1) * chunk, :] = field_ref[
                opposite(part, parts), c * chunk : (c + 1) * chunk, :
            ]


def finish(field, after):
    parts, height, cols = field.shape
    return pl.pallas_call(
        finish_kernel,
        out_shape=struct(3, parts * height // 3, cols),
        in_specs=[whole(), anywhere()],
        out_specs=whole(),
        compiler_params=params(4),
        cost_estimate=cost(0.7),
        name="finish",
    )(field, after)


def shards(cot_u, cot_v, cot_t, levels, mixing, pattern_x, blocks_x, pattern_y, blocks_y):
    depth, rows, cols = cot_u.shape
    nx, ny = (lax.axis_size("gx"), lax.axis_size("gy"))
    up_x = [(i, (i + 1) % nx) for i in range(nx)]
    down_x = [(j, i) for i, j in up_x]
    up_y = [(i, (i + 1) % ny) for i in range(ny)]
    down_y = [(j, i) for i, j in up_y]
    halfway = [[(i + nx // 2) % nx for i in range(nx)]]

    mixing = pltpu.with_memory_space_constraint(mixing, pltpu.HBM)
    cots = tuple(pltpu.with_memory_space_constraint(c, pltpu.HBM) for c in (cot_u, cot_v, cot_t))
    level_col, level_row = edges(levels)
    level_col = lax.ppermute(level_col, "gx", up_x)
    level_row = lax.ppermute(level_row, "gy", up_y)
    packed = rims(mixing, cots)
    field, wet_c, wet_u, wet_v, east, west, north, south = surface(
        levels, level_col, level_row, packed
    )
    halo_w = lax.ppermute(east, "gx", up_x)
    halo_e = lax.ppermute(west, "gx", down_x)
    tiles = {0: field}
    bit = ny // 2
    bit = 1
    while bit < ny:
        tiles[bit] = lax.ppermute(field, "gy", [(i, i ^ bit) for i in range(ny)])
        bit *= 2
    own = [m for m in tiles if m]
    *received, halo_w, halo_e = lax.optimization_barrier(
        (*(tiles[m] for m in own), halo_w, halo_e)
    )
    tiles.update(zip(own, received))
    bit = ny // 4
    while bit:
        for m in sorted(m for m in tiles if m and m % (2 * bit) == 0):
            tiles[m ^ bit] = lax.ppermute(tiles[m], "gy", [(i, i ^ bit) for i in range(ny)])
        bit //= 2
    north, south = corners(north, south, halo_e, halo_w)
    halo_s = lax.ppermute(north, "gy", up_y)
    halo_n = lax.ppermute(south, "gy", down_y)
    mixed = meridional(pattern_y, blocks_y, [tiles[m] for m in range(ny)], nx)
    mixed, halo_s, halo_n = lax.optimization_barrier((mixed, halo_s, halo_n))
    lines = lax.all_to_all(mixed, "gx", 0, 0, axis_index_groups=halfway)
    planes = (wet_c, wet_u, wet_v, mixing)
    halo_n, halo_s = (
        pltpu.with_memory_space_constraint(halo, pltpu.HBM) for halo in (halo_n, halo_s)
    )
    halos = (halo_w, halo_e, halo_n, halo_s)
    grads, state = adjoint(planes, halos, cots, mixed, rows * ny)
    turned = zonal(pattern_x, blocks_x, lines, state[0])
    back = lax.all_to_all(turned, "gx", 0, 0, axis_index_groups=halfway)
    grads = tuple(pltpu.with_memory_space_constraint(g, pltpu.HBM) for g in grads)
    grads, token = adjoint(planes, halos, cots, turned, rows * ny, (grads, state))
    return (*grads, finish(back, token[0]))


def solution(mesh):
    grid = P(None, "gy", "gx")
    flat = P("gy", "gx")
    return jax.shard_map(
        shards,
        mesh=mesh,
        in_specs=(grid, grid, grid, flat, flat, P(), P(), P(), P()),
        out_specs=(grid, grid, grid, grid),
        check_vma=False,
    )
```

```python
import functools

import jax
import jax.numpy as jnp
from jax import lax
from jax.experimental import pallas as pl
from jax.experimental.pallas import tpu as pltpu
from jax.sharding import PartitionSpec as P

time_step = 0.5
gravity_scale = 0.05
coriolis_base = 0.4
zonal_slope = 0.3
north_slope = 0.2

LANES = 128
GROUP = 8
F32 = jnp.float32
BF16 = jnp.bfloat16
MIB = 1024 * 1024
BAND = 32


def whole():
    return pl.BlockSpec(memory_space=pltpu.VMEM)


def anywhere():
    return pl.BlockSpec(memory_space=pl.ANY)


def full(*shape):
    return pl.BlockSpec(shape, lambda i: (0,) * len(shape))


def smem():
    return pl.BlockSpec(memory_space=pltpu.SMEM)


def struct(*shape):
    return jax.ShapeDtypeStruct(shape, F32)


def params(mib):
    return pltpu.CompilerParams(vmem_limit_bytes=mib * MIB)


def cost(microseconds):
    return pl.CostEstimate(
        flops=int(microseconds * 1e6), bytes_accessed=int(microseconds * 3.0e6), transcendentals=0
    )


def has_before(axis):
    return lax.axis_index(axis) > 0


def has_after(axis):
    return lax.axis_index(axis) < lax.axis_size(axis) - 1


def opposite(part, parts):
    return (part + parts - parts // 2 + 1) % parts


def lane_ids(shape):
    return lax.broadcasted_iota(jnp.int32, shape, 1)


def row_ids(shape):
    return lax.broadcasted_iota(jnp.int32, shape, 0)


def edge_kernel(levels_ref, col_ref, row_ref):
    rows, cols = levels_ref.shape
    field = levels_ref[...].astype(F32)
    col_ref[...] = jnp.transpose(field)[cols - GROUP :]
    row_ref[...] = field[rows - GROUP :]


def edges(levels):
    rows, cols = levels.shape
    return pl.pallas_call(
        edge_kernel,
        grid=(1,),
        out_shape=(struct(GROUP, rows), struct(GROUP, cols)),
        in_specs=[full(rows, cols)],
        out_specs=(full(GROUP, rows), full(GROUP, cols)),
        compiler_params=params(4),
        cost_estimate=cost(1.0),
        name="edges",
    )(levels)


def rim_kernel(
    step,
    mix_ref,
    u_ref,
    v_ref,
    t_ref,
    east_ref,
    west_ref,
    north_ref,
    south_ref,
    top_ref,
    u_here,
    v_here,
    t_here,
    arrived,
):
    depth, rows, cols = u_ref.shape
    fields = ((u_ref, u_here), (v_ref, v_here), (t_ref, t_here))
    chunk = 2 * GROUP
    lane = lane_ids((chunk, cols))
    edge = (lane == 0) | (lane == cols - 1)

    def copy(f, at):
        levels = pl.ds(at * step, step)
        source, target = fields[f]
        return pltpu.make_async_copy(source.at[levels], target.at[levels], arrived.at[f, at])

    for at in range(depth // step):
        for f in range(3):
            copy(f, at).start()
    east_ref[...] = jnp.zeros((rows, cols), F32)
    west_ref[...] = jnp.zeros((rows, cols), F32)
    mix = mix_ref[...]
    rest = north_ref.shape[0] - 3 * BAND
    north_ref[3 * BAND :, :] = jnp.broadcast_to(mix[rows - 1 :], (rest, cols))
    south_ref[3 * BAND :, :] = jnp.broadcast_to(mix[:1], (rest, cols))

    def levels(at, carry):
        first = at * step
        flip = lax.rem(first, 2) == 1
        for f in range(3):
            copy(f, at).wait()

        def body(i, inner):
            here = pl.ds(pl.multiple_of(i * chunk, chunk), chunk)
            sums = [None, None]
            for k in range(step):
                for f in range(3):
                    value = jnp.where(edge, fields[f][1][first + k, here, :], 0.0)
                    moved = pltpu.roll(value, BAND * f + first + k + 1, 1)
                    sums[k % 2] = moved if sums[k % 2] is None else sums[k % 2] + moved
            east_ref[here, :] += jnp.where(flip, sums[1], sums[0])
            west_ref[here, :] += jnp.where(flip, sums[0], sums[1])
            return inner

        lax.fori_loop(0, rows // chunk, body, 0, unroll=8)
        return carry

    lax.fori_loop(0, depth // step, levels, 0)
    ids = lane_ids((rows, cols))
    even = lax.rem(ids, 2) == 0
    mix = pltpu.roll(mix, 3 * BAND + 1, 1)
    even_levels = east_ref[...]
    odd_levels = west_ref[...]
    east = jnp.where(even, even_levels, odd_levels)
    west = jnp.where(even, odd_levels, even_levels)
    east_ref[...] = jnp.where(ids == 3 * BAND, mix, east)
    west_ref[...] = jnp.where(ids == 3 * BAND + 1, mix, west)
    empty = jnp.zeros((BAND - depth, cols), F32)
    for f in range(3):
        band = slice(f * BAND, (f + 1) * BAND)
        here = fields[f][1]
        for out, place in ((north_ref, rows - 1), (south_ref, 0)):
            line = here[:, place : place + 1, :].reshape(depth, cols)
            out[band, :] = jnp.concatenate([line, empty], axis=0)
        top_ref[f] = here[0]


def rims(mixing, cots):
    depth, rows, cols = cots[0].shape
    step = 5
    lines = 3 * BAND + GROUP
    return pl.pallas_call(
        functools.partial(rim_kernel, step),
        out_shape=(struct(rows, cols),) * 2
        + (struct(lines, cols),) * 2
        + (struct(3, rows, cols),),
        in_specs=[whole()] + [anywhere()] * 3,
        out_specs=(whole(),) * 5,
        scratch_shapes=[pltpu.VMEM((depth, rows, cols), F32)] * 3
        + [pltpu.SemaphoreType.DMA((3, depth // step))],
        compiler_params=params(14),
        cost_estimate=cost(6.0),
        name="rims",
    )(mixing, *cots)


def surface_kernel(
    levels_ref,
    col_ref,
    row_ref,
    east_ref,
    west_ref,
    north_ref,
    south_ref,
    top_ref,
    out_ref,
    wet_c_ref,
    wet_u_ref,
    wet_v_ref,
    east_out_ref,
    west_out_ref,
    north_out_ref,
    south_out_ref,
):
    rows, cols = levels_ref.shape
    field = levels_ref[...].astype(F32)
    lane = lane_ids(field.shape)
    row = row_ids(field.shape)
    col = jnp.broadcast_to(jnp.transpose(col_ref[...])[:, GROUP - 1 :], field.shape)
    col = jnp.where(has_before("gx"), col, 0.0)
    west = jnp.where(lane == 0, col, pltpu.roll(field, 1, 1))
    line = jnp.broadcast_to(row_ref[GROUP - 1 :, :], field.shape)
    line = jnp.where(has_before("gy"), line, 0.0)
    south = jnp.where(row == 0, line, pltpu.roll(field, 1, 0))
    wet_u = jnp.minimum(field, west)
    wet_v = jnp.minimum(field, south)
    wets = (wet_u, wet_v, field)
    wet_c_ref[...] = field
    wet_u_ref[...] = wet_u
    wet_v_ref[...] = wet_v
    for comp in range(3):
        out_ref[comp] = jnp.where(wets[comp] > 0.0, time_step * top_ref[comp], 0.0)
    for ref, out, place, shift in (
        (east_ref, east_out_ref, cols - 1, 0),
        (west_ref, west_out_ref, 0, 1),
    ):
        at = lax.rem(lane + cols - shift, cols)
        band = at // BAND
        level = lax.rem(at, BAND).astype(F32)
        limit = [jnp.broadcast_to(wet[:, place : place + 1], field.shape) for wet in wets]
        limit = jnp.where(band == 0, limit[0], jnp.where(band == 1, limit[1], limit[2]))
        out[...] = jnp.where((level < limit) | (band == 3), ref[...], 0.0)
    level = row_ids((BAND, cols)).astype(F32)
    for ref, out, place in ((north_ref, north_out_ref, rows - 1), (south_ref, south_out_ref, 0)):
        out[3 * BAND :, :] = ref[3 * BAND :, :]
        for f in range(3):
            band = slice(f * BAND, (f + 1) * BAND)
            out[band, :] = jnp.where(level < wets[f][place : place + 1], ref[band, :], 0.0)


def surface(levels, col, row, packed):
    rows, cols = levels.shape
    rim = tuple(struct(*value.shape) for value in packed[:4])
    return pl.pallas_call(
        surface_kernel,
        out_shape=(struct(3, rows, cols),) + (struct(rows, cols),) * 3 + rim,
        in_specs=[whole()] * 8,
        out_specs=(whole(),) * 8,
        compiler_params=params(4),
        cost_estimate=cost(1.5),
        name="surface",
    )(levels, col, row, *packed)


def corner_kernel(north_ref, south_ref, east_ref, west_ref, north_out_ref, south_out_ref):
    spot = row_ids(north_ref.shape) == 3 * BAND + 1
    last = east_ref.shape[0] - 1
    corner = jnp.broadcast_to(east_ref[last:, :], north_ref.shape)
    north_out_ref[...] = jnp.where(spot, corner, north_ref[...])
    corner = jnp.broadcast_to(west_ref[:1, :], south_ref.shape)
    south_out_ref[...] = jnp.where(spot, corner, south_ref[...])


def corners(north, south, halo_e, halo_w):
    return pl.pallas_call(
        corner_kernel,
        out_shape=(struct(*north.shape),) * 2,
        in_specs=[whole()] * 4,
        out_specs=(whole(),) * 2,
        compiler_params=params(4),
        cost_estimate=cost(0.3),
        name="corners",
    )(north, south, halo_e, halo_w)


def adjoint_kernel(
    step,
    done,
    depth,
    total_rows,
    wet_c_ref,
    wet_u_ref,
    wet_v_ref,
    mix_ref,
    hw_ref,
    he_ref,
    hn_ref,
    hs_ref,
    old_refs,
    u_ref,
    v_ref,
    t_ref,
    gu_ref,
    gv_ref,
    gt_ref,
    state_ref,
    mix_n_ref,
    mix_s_ref,
    keep_ref,
    cor_ref,
    a_ref,
    b_ref,
    c_ref,
):
    rows, cols = mix_ref.shape
    at = pl.program_id(0)
    half = depth // 2
    first = depth - (done + at + 1) * step
    pad = GROUP
    cor_step = 0.25 * time_step * coriolis_base / total_rows
    slope_u = 0.5 * time_step * zonal_slope
    slope_v = 0.5 * time_step * north_slope
    weight = time_step * gravity_scale
    before_y, after_y = (has_before("gy"), has_after("gy"))

    @pl.when(at == 0)
    def _():
        shape = (rows, cols)
        lane = lane_ids(shape)
        row = row_ids(shape)
        start = lax.axis_index("gy") * rows
        lines = (row + start).astype(F32)
        cor = (0.25 * time_step * coriolis_base) * (0.5 + (lines + 0.5) / total_rows)
        cor_n = (0.25 * time_step * coriolis_base) * (0.5 + (lines + 1.5) / total_rows)
        cor_s = (0.25 * time_step * coriolis_base) * (0.5 + (lines - 0.5) / total_rows)
        cor_ref[...] = cor
        mix = mix_ref[...]
        keep_ref[...] = 1.0 - 4.0 * mix
        mix_n_ref[...] = jnp.where(
            row == rows - 1,
            jnp.broadcast_to(jnp.where(after_y, hn_ref[3 * BAND : 3 * BAND + 1, :], 0.0), shape),
            pltpu.roll(mix, rows - 1, 0),
        )
        mix_s_ref[...] = jnp.where(
            row == 0,
            jnp.broadcast_to(jnp.where(before_y, hs_ref[3 * BAND : 3 * BAND + 1, :], 0.0), shape),
            pltpu.roll(mix, 1, 0),
        )
        if old_refs:
            state_ref[...] = old_refs[0][...]
            return
        east = jnp.where(has_after("gx"), he_ref[...], 0.0)
        corner = hs_ref[3 * BAND + 1 : 3 * BAND + 2, :]
        corner = jnp.where(has_after("gx") & before_y, corner, 0.0)
        kind = lax.rem(lane + cols - 1, cols) // BAND
        mixed = east * jnp.broadcast_to(east[:, 3 * BAND + 1 : 3 * BAND + 2], shape)
        below = jnp.where(
            row == 0,
            jnp.broadcast_to(corner, shape),
            pltpu.roll(east, 1, 0),
        )
        turned = cor * east + cor_s * below
        total = jnp.where(kind == 0, east, 0.0)
        reach = 1
        while reach < depth:
            total = total + pltpu.roll(total, cols - reach, 1)
            reach *= 2
        from_e = (
            mixed
            + jnp.where(kind == 1, pltpu.roll(turned, BAND, 1), 0.0)
            + jnp.where(kind == 2, pltpu.roll(weight * total, 2 * BAND, 1), 0.0)
        )
        west = jnp.where(has_before("gx"), hw_ref[...], 0.0)
        corner = hn_ref[3 * BAND + 1 : 3 * BAND + 2, :]
        corner = jnp.where(has_before("gx") & after_y, corner, 0.0)
        kind = lane // BAND
        mixed = west * jnp.broadcast_to(west[:, 3 * BAND : 3 * BAND + 1], shape)
        above = jnp.where(
            row == rows - 1,
            jnp.broadcast_to(corner, shape),
            pltpu.roll(west, rows - 1, 0),
        )
        turned = cor * west + cor_n * above
        from_w = mixed - jnp.where(
            kind == 0,
            pltpu.roll(turned, cols - BAND, 1) + pltpu.roll(slope_u * west, cols - 2 * BAND, 1),
            0.0,
        )
        both = jnp.concatenate([from_e, from_w], axis=1)
        source = row_ids((2 * cols, 2 * cols))
        place = lane_ids((2 * cols, 2 * cols))
        part = place // cols
        spot = lax.rem(place, cols)
        pair = spot // 2
        slot = BAND * (pair // half) + part * half + lax.rem(pair, half)
        wanted = jnp.where(lax.rem(spot, 2) == 0, slot + 1, slot + cols)
        moves = jnp.where((source == wanted) & (pair < 3 * half), 1.0, 0.0).astype(BF16)
        moved = jnp.zeros((rows, 2 * cols), F32)
        for _ in range(3):
            high = both.astype(BF16)
            both = both - high.astype(F32)
            moved = moved + jnp.dot(high, moves, preferred_element_type=F32)
        state_ref[0] = moved[:, :cols]
        state_ref[1] = moved[:, cols:]
        state_ref[2] = jnp.zeros(shape, F32)
        state_ref[3] = jnp.zeros(shape, F32)

    fields = (
        (u_ref, wet_u_ref, a_ref),
        (v_ref, wet_v_ref, b_ref),
        (t_ref, wet_c_ref, c_ref),
    )

    def mask(i, carry):
        base = pl.multiple_of(i * 2 * GROUP, 2 * GROUP)
        here = pl.ds(base, 2 * GROUP)
        there = pl.ds(pl.multiple_of(base + pad, GROUP), 2 * GROUP)
        wets = [wet[here, :] for _, wet, _ in fields]
        for k in range(step):
            level = (first + k).astype(F32)
            for f, (ref, _, out) in enumerate(fields):
                out[k, there, :] = jnp.where(level < wets[f], ref[k, here, :], 0.0)
        return carry

    lax.fori_loop(0, rows // (2 * GROUP), mask, 0, unroll=8)
    for k in range(step):
        for f, (_, _, out) in enumerate(fields):
            slot = BAND * f + first + k
            out[k, pad - 1 : pad, :] = jnp.where(before_y, hs_ref[pl.ds(slot, 1), :], 0.0)
            out[k, pad + rows : pad + rows + 1, :] = jnp.where(
                after_y, hn_ref[pl.ds(slot, 1), :], 0.0
            )

    chunk = 2 * GROUP
    lane = lane_ids((chunk, cols))
    is_east = lane == cols - 1
    is_west = lane == 0
    part = (first >= half).astype(jnp.int32)

    def body(i, carry):
        base = pl.multiple_of(i * chunk, chunk)
        here = pl.ds(base, chunk)
        center = pl.ds(base + pad, chunk)
        north = pl.ds(base + pad + 1, chunk)
        south = pl.ds(base + pad - 1, chunk)
        mix = mix_ref[here, :]
        mix_n = mix_n_ref[here, :]
        mix_s = mix_s_ref[here, :]
        keep = keep_ref[here, :]
        cor = cor_ref[here, :]
        cor_n = cor + cor_step
        cor_s = cor - cor_step
        edges = state_ref[part, here, :]
        sum_a = state_ref[2, here, :]
        sum_d = state_ref[3, here, :]
        for k in reversed(range(step)):
            inner = first + k - part * half

            def both_sides(west, east, f, inner=inner):
                edge = pltpu.roll(edges, 2 * cols - 1 - 2 * (f * half + inner), 1)
                return jnp.where(is_west, edge, pltpu.roll(west, 1, 1)) + jnp.where(
                    is_east, edge, pltpu.roll(east, cols - 1, 1)
                )

            a = a_ref[k, center, :]
            a_n = a_ref[k, north, :]
            a_s = a_ref[k, south, :]
            b = b_ref[k, center, :]
            b_n = b_ref[k, north, :]
            b_s = b_ref[k, south, :]
            c = c_ref[k, center, :]
            c_n = c_ref[k, north, :]
            c_s = c_ref[k, south, :]
            mix_a = mix * a
            turn_b = cor * b + cor_n * b_n + slope_u * c
            gu_ref[k, here, :] = (
                keep * a
                + (mix_n * a_n + mix_s * a_s)
                - turn_b
                + both_sides(mix_a - turn_b, mix_a, 0)
            )
            mix_b = mix * b
            turn_a = cor * a + cor_s * a_s
            gv_ref[k, here, :] = (
                keep * b
                + (mix_n * b_n + mix_s * b_s)
                + (turn_a - slope_v * (c + c_s))
                + both_sides(mix_b, mix_b + turn_a, 1)
            )
            mix_c = mix * c
            sum_a = sum_a + weight * a
            sum_d = sum_d + weight * (b - b_n)
            gt_ref[k, here, :] = (
                keep * c
                + (mix_n * c_n + mix_s * c_s)
                - (sum_a + sum_d)
                + both_sides(mix_c, mix_c + sum_a, 2)
            )
        state_ref[2, here, :] = sum_a
        state_ref[3, here, :] = sum_d
        return carry

    lax.fori_loop(0, rows // chunk, body, 0, unroll=rows // chunk)


def adjoint(planes, halos, cots, after, total_rows, earlier=None):
    depth, rows, cols = cots[0].shape
    step = 5
    first = depth // (2 * step)
    done, steps = (0, first) if earlier is None else (first, depth // step - first)
    plane = full(rows, cols)
    top = depth // step - 1 - done
    block = pl.BlockSpec((step, rows, cols), lambda i: (top - i, 0, 0))
    grads, state = ((), ()) if earlier is None else earlier
    n_planes = len(planes) + len(halos)
    n_state = len(state)
    kept = (4, rows, cols)

    def kernel(*refs):
        front, refs = refs[:n_planes], refs[n_planes:]
        old, refs = refs[:n_state], refs[n_state:]
        ins, refs = refs[:3], refs[3 + 1 + len(grads) :]
        adjoint_kernel(step, done, depth, total_rows, *front, old, *ins, *refs)

    padded = pltpu.VMEM((step, rows + 2 * GROUP, cols), F32)
    aliases = {n_planes + n_state + 4 + i: i for i in range(len(grads))}
    result = pl.pallas_call(
        kernel,
        grid=(steps,),
        out_shape=(struct(depth, rows, cols),) * 3 + (struct(*kept),),
        in_specs=[plane] * len(planes)
        + [full(*halo.shape) for halo in halos]
        + [full(*kept)] * n_state
        + [block] * 3
        + [anywhere()] * (1 + len(grads)),
        out_specs=(block,) * 3 + (full(*kept),),
        scratch_shapes=[pltpu.VMEM((rows, cols), F32)] * 4 + [padded] * 3,
        input_output_aliases=aliases,
        compiler_params=params(16),
        cost_estimate=cost(3.0 * steps),
        name="adjoint",
    )(*planes, *halos, *state, *cots, after, *grads)
    return result[:3], result[3:]


def halves(value):
    high = value.astype(BF16)
    return high, (value - high.astype(F32)).astype(BF16)


def product(blocks, fields, field_first):
    axis = 1 if field_first else 0
    block_high, block_low = (jnp.concatenate([b[i] for b in blocks], axis=1) for i in range(2))
    field_high, field_low = (jnp.concatenate([f[i] for f in fields], axis=axis) for i in range(2))
    if field_first:
        first, second = (field_high, field_low), (block_high, block_low)
    else:
        first, second = (block_high, block_low), (field_high, field_low)
    dims = (((1,), (axis,)), ((), ()))
    both = lax.dot_general(
        jnp.concatenate(first, axis=0), second[0], dims, preferred_element_type=F32
    )
    last = lax.dot_general(first[0], second[1], dims, preferred_element_type=F32)
    size = first[0].shape[0]
    return both[:size] + (both[size:] + last)


def zonal_kernel(pattern_ref, blocks_ref, field_ref, after_ref, out_ref, high_ref, low_ref):
    for slot in range(field_ref.shape[0]):
        tile = (slot + field_ref.shape[0] // 2 - 1) % field_ref.shape[0]
        high_ref[tile], low_ref[tile] = halves(field_ref[slot])
    for r in range(blocks_ref.shape[0]):
        entries = range(blocks_ref.shape[1])
        picked = [pattern_ref[r, j] for j in entries]
        out_ref[opposite(r, out_ref.shape[0])] = product(
            [halves(blocks_ref[r, j]) for j in entries],
            [(high_ref[p], low_ref[p]) for p in picked],
            True,
        )


def zonal(pattern, blocks, field, after):
    return pl.pallas_call(
        zonal_kernel,
        out_shape=struct(*field.shape),
        in_specs=[smem()] + [whole()] * 2 + [anywhere()],
        out_specs=whole(),
        scratch_shapes=[pltpu.VMEM(field.shape, BF16)] * 2,
        compiler_params=params(6),
        cost_estimate=cost(2.0),
        name="zonal",
    )(pattern, blocks, field, after)


def meridional_kernel(pattern_ref, blocks_ref, field_refs, out_ref, high_ref, low_ref):
    _, block, _ = high_ref.shape
    _, rows, cols = field_refs[0].shape
    chunk = out_ref.shape[1] // 3
    mine = rows // block
    me = lax.axis_index("gy")
    for m, ref in enumerate(field_refs):
        first = (me ^ m) * mine
        for h in range(mine):
            here = slice(h * block, (h + 1) * block)
            value = jnp.concatenate([ref[c, here, :] for c in range(3)], axis=1)
            high_ref[first + h], low_ref[first + h] = halves(value)
    entries = range(blocks_ref.shape[1])
    for h in range(mine):
        r = me * mine + h
        picked = [pattern_ref[r, j] for j in entries]
        result = product(
            [halves(blocks_ref[r, j]) for j in entries],
            [(high_ref[p], low_ref[p]) for p in picked],
            False,
        )
        for line in range(0, block, chunk):
            part = (h * block + line) // chunk
            for c in range(3):
                out_ref[opposite(part, out_ref.shape[0]), c * chunk : (c + 1) * chunk, :] = result[
                    line : line + chunk, c * cols : (c + 1) * cols
                ]


def meridional(pattern, blocks, fields, parts):
    n = len(fields)
    _, rows, cols = fields[0].shape
    tiles, _, block, _ = blocks.shape

    def kernel(pattern_ref, blocks_ref, *refs):
        meridional_kernel(pattern_ref, blocks_ref, refs[:n], *refs[n:])

    return pl.pallas_call(
        kernel,
        out_shape=struct(parts, 3 * rows // parts, cols),
        in_specs=[smem()] + [whole()] * (1 + n),
        out_specs=whole(),
        scratch_shapes=[pltpu.VMEM((tiles, block, 3 * cols), BF16)] * 2,
        compiler_params=params(4 + n),
        cost_estimate=cost(2.0),
        name="meridional",
    )(pattern, blocks, *fields)


def finish_kernel(field_ref, after_ref, out_ref):
    parts, height, cols = field_ref.shape
    chunk = height // 3
    for part in range(parts):
        for c in range(3):
            out_ref[c, part * chunk : (part + 1) * chunk, :] = field_ref[
                opposite(part, parts), c * chunk : (c + 1) * chunk, :
            ]


def finish(field, after):
    parts, height, cols = field.shape
    return pl.pallas_call(
        finish_kernel,
        out_shape=struct(3, parts * height // 3, cols),
        in_specs=[whole(), anywhere()],
        out_specs=whole(),
        compiler_params=params(4),
        cost_estimate=cost(0.7),
        name="finish",
    )(field, after)


def shards(cot_u, cot_v, cot_t, levels, mixing, pattern_x, blocks_x, pattern_y, blocks_y):
    depth, rows, cols = cot_u.shape
    nx, ny = (lax.axis_size("gx"), lax.axis_size("gy"))
    up_x = [(i, (i + 1) % nx) for i in range(nx)]
    down_x = [(j, i) for i, j in up_x]
    up_y = [(i, (i + 1) % ny) for i in range(ny)]
    down_y = [(j, i) for i, j in up_y]
    halfway = [[(i + nx // 2 - 1) % nx for i in range(nx)]]

    mixing = pltpu.with_memory_space_constraint(mixing, pltpu.HBM)
    cots = tuple(pltpu.with_memory_space_constraint(c, pltpu.HBM) for c in (cot_u, cot_v, cot_t))
    level_col, level_row = edges(levels)
    level_col = lax.ppermute(level_col, "gx", up_x)
    level_row = lax.ppermute(level_row, "gy", up_y)
    packed = rims(mixing, cots)
    field, wet_c, wet_u, wet_v, east, west, north, south = surface(
        levels, level_col, level_row, packed
    )
    halo_w = lax.ppermute(east, "gx", up_x)
    halo_e = lax.ppermute(west, "gx", down_x)
    tiles = {0: field}
    bit = ny // 2
    bit = 1
    while bit < ny:
        tiles[bit] = lax.ppermute(field, "gy", [(i, i ^ bit) for i in range(ny)])
        bit *= 2
    own = [m for m in tiles if m]
    *received, halo_w, halo_e = lax.optimization_barrier(
        (*(tiles[m] for m in own), halo_w, halo_e)
    )
    tiles.update(zip(own, received))
    bit = ny // 4
    while bit:
        for m in sorted(m for m in tiles if m and m % (2 * bit) == 0):
            tiles[m ^ bit] = lax.ppermute(tiles[m], "gy", [(i, i ^ bit) for i in range(ny)])
        bit //= 2
    north, south = corners(north, south, halo_e, halo_w)
    halo_s = lax.ppermute(north, "gy", up_y)
    halo_n = lax.ppermute(south, "gy", down_y)
    mixed = meridional(pattern_y, blocks_y, [tiles[m] for m in range(ny)], nx)
    mixed, halo_s, halo_n = lax.optimization_barrier((mixed, halo_s, halo_n))
    lines = lax.all_to_all(mixed, "gx", 0, 0, axis_index_groups=halfway)
    planes = (wet_c, wet_u, wet_v, mixing)
    halo_n, halo_s = (
        pltpu.with_memory_space_constraint(halo, pltpu.HBM) for halo in (halo_n, halo_s)
    )
    halos = (halo_w, halo_e, halo_n, halo_s)
    grads, state = adjoint(planes, halos, cots, mixed, rows * ny)
    turned = zonal(pattern_x, blocks_x, lines, state[0])
    back = lax.all_to_all(turned, "gx", 0, 0, axis_index_groups=halfway)
    grads = tuple(pltpu.with_memory_space_constraint(g, pltpu.HBM) for g in grads)
    grads, token = adjoint(planes, halos, cots, turned, rows * ny, (grads, state))
    return (*grads, finish(back, token[0]))


def solution(mesh):
    grid = P(None, "gy", "gx")
    flat = P("gy", "gx")
    return jax.shard_map(
        shards,
        mesh=mesh,
        in_specs=(grid, grid, grid, flat, flat, P(), P(), P(), P()),
        out_specs=(grid, grid, grid, grid),
        check_vma=False,
    )
```
